32 devices in a mesh: dp: 4 (over y, x), expert: 8 (over z, core).
Axes of the slice: x: 2, y: 2, z: 4, core: 2. Of those that a mesh axis runs over, the one named last changes fastest.
Arguments:
- tokens: bfloat16 [32768, 768], P(('dp', 'expert')), may hold values from -6 to 6
- cotangent: bfloat16 [32768, 768], P(('dp', 'expert')), may hold values from -6 to 6
- routes: int32 [32768, 1], P(('dp', 'expert')), may hold values from 0 to 7
- seq_len: int32 [64], P(('dp', 'expert')), may hold values from 106 to 512
- buckets: int32 [512, 512], replicated, may hold values from 0 to 31, as said below
- w_qkv: bfloat16 [768, 2304], replicated, may hold values from -0.21875 to 0.21875
- w_out_proj: bfloat16 [768, 768], replicated, may hold values from -4 to 4
- rel_bias: float32 [32, 12], replicated, may hold values from -4 to 4
- gain_attn: float32 [768], replicated, may hold values from 0.5 to 1.5
- gain_ffn: float32 [768], replicated, may hold values from 0.5 to 1.5
- router: float32 [768, 8], replicated, may hold values from -0.375 to 0.375
- w_in: bfloat16 [8, 768, 3072], P('expert'), may hold values from -0.21875 to 0.21875
- w_out: bfloat16 [8, 3072, 768], P('expert'), may hold values from -3 to 3
Outputs:
- output: bfloat16 [32768, 768], P(('dp', 'expert'))
- grad_tokens: float32 [32768, 768], P(('dp', 'expert'))
- grad_qkv: float32 [768, 2304], replicated
- grad_out_proj: float32 [768, 768], replicated
- grad_rel_bias: float32 [32, 12], replicated
- grad_gain_attn: float32 [768], replicated
- grad_gain_ffn: float32 [768], replicated
- grad_router: float32 [768, 8], replicated
- grad_w_in: float32 [8, 768, 3072], P('expert', None, 'dp')
- grad_w_out: float32 [8, 3072, 768], P('expert', 'dp')
- balance_loss: float32 [], replicated
The draws below stay inside these ranges and needn't reach their ends.
Inputs may be any that keep to these rules, and one draw needn't show every extreme that they name: The entry at row i, column j depends only on j - i: T5's bidirectional bucketing, offsets below 8 exact, longer ones in buckets growing geometrically up to 128, positive offsets in buckets of their own; the bucket labels come in a drawn order.
All inputs are finite; a program needn't handle non-finite values.
Results may differ from the reference program's by a relative error of at most 0.017.
Values may be sent and summed in bfloat16 or wider, within the bound.
No kernel may reach another device: no remote copies, remote signals or barrier semaphores. Data moves between devices by JAX's collectives and lax.ppermute only.
A program may use at most 256 MiB of HBM per device.

```python
import math
from functools import partial
import jax
import jax.numpy as jnp
from jax import lax

D = 768
HEADS = 12
HEAD_DIM = 64
FF = 3072
BUCKETS = 32
MAX_DISTANCE = 128
LEN = 512
TOK_DEV = 1024
SEQS = 64
TOKENS = 32768
EXPERTS = 8
CAP = 160


def draw_buckets(key, part):
    key = jax.random.fold_in(key, 7)
    half_count = BUCKETS // 2
    exact_count = half_count // 2
    limits = [math.ceil(exact_count * (MAX_DISTANCE / exact_count) ** (section / exact_count) - 1e-09) for section in range(1, exact_count)]
    positions = jnp.arange(LEN, dtype=jnp.int32)
    offsets = positions[None, :] - positions[:, None]
    distance = jnp.abs(offsets)
    far_part = exact_count + sum(((distance >= border).astype(jnp.int32) for border in limits))
    within = jnp.where(distance < exact_count, distance, jnp.minimum(far_part, half_count - 1))
    bucket_ids = within + half_count * (offsets > 0).astype(jnp.int32)
    labels = jax.random.permutation(key, BUCKETS).astype(jnp.int32)
    return labels[bucket_ids]


def draw_seq_len(key, part):
    key = jax.random.fold_in(key, 11)
    index = jnp.arange(SEQS, dtype=jnp.int32)
    base = LEN // 3 + 2 * LEN * index // (3 * max(SEQS - 1, 1))
    jitter = jax.random.randint(key, (SEQS,), -(LEN // 8), LEN // 8 + 1).astype(jnp.int32)
    lengths = jnp.clip(base + jitter, max(1, LEN // 3 - LEN // 8), LEN)
    lengths = jnp.where(index == 0, max(1, LEN // 3 - LEN // 8), lengths)
    lengths = jnp.where(index == SEQS - 1, LEN, lengths)
    return lengths.astype(jnp.int32)


def block_scale(rng, shape, shards, low, largest):
    def one(dim, blocks):
        steps = jax.random.uniform(jax.random.fold_in(jax.random.fold_in(rng, 6), dim), (blocks,), jnp.float32, low / len(shards), largest / len(shards))
        return jnp.repeat(jnp.exp(steps), shape[dim] // blocks).reshape((-1,) + (1,) * (len(shape) - dim - 1))

    level = one(*shards[0])
    for cut in shards[1:]:
        level = level * one(*cut)
    return level


def different_ones(own_key, rows, amount, top, lift):
    sequence = jax.random.permutation(jax.random.fold_in(own_key, 1), amount)
    boost = sequence
    for power in range(3):
        boost = boost * boost // amount
    boost = boost * lift // amount
    lots = jax.random.randint(jax.random.fold_in(own_key, 2), (rows, amount), 0, 4096) + boost
    holders = jax.random.permutation(jax.random.fold_in(own_key, 3), rows)[jnp.arange(amount) % rows]
    lots = jnp.where(jnp.arange(rows)[:, None] == holders[None, :], 1 << 14, lots)
    merit = lots * amount + jnp.arange(amount)
    return lax.top_k(merit.astype(jnp.int32), top)[1].astype(jnp.int32)


def noise(own_key, extent, spread, most, split=(), kind=jnp.bfloat16):
    values = jax.random.normal(own_key, extent, jnp.float32) * spread
    if len(split) > 0:
        values = block_scale(own_key, extent, split, -0.22, 0.18) * values
    return jnp.clip(values, min=-most, max=most).astype(kind)


def setup_inputs(seed: int = 0) -> dict:
    streams_of = jax.random.split(jax.random.key(seed), 14)
    tokens = noise(streams_of[0], (TOKENS, D), 1.0, 6.0, ((0, 32),))
    cotangent = noise(streams_of[1], (TOKENS, D), 1.0, 6.0, ((0, 32),))
    routes = different_ones(streams_of[2], TOKENS, EXPERTS, 1, 1024)
    seq_len = draw_seq_len(jax.random.fold_in(streams_of[13], 71), 0)
    buckets = draw_buckets(jax.random.fold_in(streams_of[13], 71), 0)
    w_qkv = noise(streams_of[5], (D, 3 * D), D ** -0.5, 0.21875)
    w_out_proj = noise(streams_of[6], (D, D), (8 * D ** -0.5), 4.0)
    rel_bias = noise(streams_of[7], (BUCKETS, HEADS), 1.0, 4.0, (), jnp.float32)
    gain_attn = jnp.clip(1.0 + 0.1 * jax.random.normal(streams_of[8], (D,), jnp.float32), 0.5, 1.5)
    gain_ffn = jnp.clip(1.0 + 0.1 * jax.random.normal(streams_of[9], (D,), jnp.float32), 0.5, 1.5)
    router = noise(streams_of[10], (D, EXPERTS), (0.7 * D ** -0.5), 0.375, (), jnp.float32)
    w_in = noise(streams_of[11], (EXPERTS, D, FF), D ** -0.5, 0.21875, ((0, 8),))
    w_out = noise(streams_of[12], (EXPERTS, FF, D), (EXPERTS * 2 ** 0.5 * FF ** -0.5), 3.0, ((0, 8),))
    return dict(tokens=tokens, cotangent=cotangent, routes=routes, seq_len=seq_len, buckets=buckets, w_qkv=w_qkv, w_out_proj=w_out_proj, rel_bias=rel_bias, gain_attn=gain_attn, gain_ffn=gain_ffn, router=router, w_in=w_in, w_out=w_out)


@jax.custom_vjp
def low(v):
    return lax.optimization_barrier(v.astype(jnp.bfloat16)).astype(jnp.float32)

@jax.custom_vjp
def low_back(v):
    return v

def low_keep(v):
    return (low(v), None)

def low_pass(kept, grad):
    return (grad,)

def back_keep(v):
    return (v, None)

def back_low(kept, grad):
    return (low(grad),)
low.defvjp(low_keep, low_pass)
low_back.defvjp(back_keep, back_low)
EPSILON = 1e-06
AUX_WEIGHT = 0.01
HIGHEST = lax.Precision.HIGHEST

def rms_norm(values, gain):
    return values * lax.rsqrt(lax.optimization_barrier(jnp.mean(values * values, axis=-1, keepdims=True)) + EPSILON) * gain

def attend(block, bias):
    queries, keys_all, values_all, lengths = block
    scores = jnp.einsum('gqhd,gkhd->ghqk', queries, keys_all, precision=HIGHEST) * HEAD_DIM ** (-0.5) + bias[None]
    scores = low_back(scores)
    usable = jnp.arange(LEN, dtype=jnp.int32)[None, :] < lengths[:, None]
    scores = jnp.where(usable[:, None, None, :], scores, -1000000000.0)
    probs = low(jax.nn.softmax(scores, axis=-1))
    return jnp.einsum('ghqk,gkhd->gqhd', probs, values_all, precision=HIGHEST)

def expert_apply(block):
    first, second, inputs = block
    hidden = low_back(jnp.dot(inputs, first, precision=HIGHEST))
    active = low(jax.nn.gelu(hidden))
    return low(low_back(jnp.dot(active, second, precision=HIGHEST)))

def reference(tokens, cotangent, routes, seq_len, buckets, w_qkv, w_out_proj, rel_bias, gain_attn, gain_ffn, router, w_in, w_out):
    devices = TOKENS // TOK_DEV
    group = math.gcd(SEQS, 8)
    valid_mask = (jnp.arange(LEN, dtype=jnp.int32)[None, :] < seq_len[:, None]).reshape(TOKENS)
    valid = valid_mask.astype(jnp.float32)
    choice_ids = routes[:, 0]
    routed_int = jnp.logical_and(choice_ids[:, None] == jnp.arange(EXPERTS, dtype=jnp.int32)[None, :], valid_mask[:, None]).astype(jnp.int32)
    routed_dev = routed_int.reshape(devices, TOK_DEV, EXPERTS)
    earlier = jnp.cumsum(routed_dev, axis=1) - routed_dev
    place = lax.optimization_barrier(jnp.sum(earlier * routed_dev, axis=2))
    is_routed = lax.optimization_barrier(jnp.sum(routed_dev, axis=2)) > 0
    is_kept = jnp.logical_and(is_routed, place < CAP)
    slot_ids = jnp.where(is_kept, choice_ids.reshape(devices, TOK_DEV) * CAP + place, EXPERTS * CAP).astype(jnp.int32)
    device_ids = jnp.broadcast_to(jnp.arange(devices, dtype=jnp.int32)[:, None], (devices, TOK_DEV)).astype(jnp.int32)
    routed = routed_int.astype(jnp.float32)
    token_total = jnp.asarray(TOKENS, dtype=jnp.float32)
    share = lax.optimization_barrier(jnp.sum(routed, axis=0)) / token_total

    def forward(inputs, qkv_weight, out_weight, bias_table, gain_a, gain_b, router_weight, first_all, second_all):
        normed_a = low(rms_norm(inputs, gain_a))
        qkv = low(low_back(jnp.dot(normed_a, qkv_weight, precision=HIGHEST)))
        qkv = qkv.reshape(SEQS // group, group, LEN, 3, HEADS, HEAD_DIM)
        bias = jnp.transpose(jnp.take(bias_table, buckets, axis=0), (2, 0, 1))
        mixed = lax.map(jax.checkpoint(partial(attend, bias=bias)), (qkv[:, :, :, 0], qkv[:, :, :, 1], qkv[:, :, :, 2], seq_len.reshape(SEQS // group, group)))
        attn = low(low_back(mixed.reshape(TOKENS, D)))
        branch = low_back(jnp.dot(attn, out_weight, precision=HIGHEST))
        middle = inputs + branch
        normed_b = low(rms_norm(middle, gain_b))
        logits = jnp.dot(normed_b, router_weight, precision=HIGHEST)
        probs = jax.nn.softmax(logits, axis=-1)
        gate = lax.optimization_barrier(jnp.sum(probs * routed, axis=1))
        buffers = jnp.zeros((devices, EXPERTS * CAP + 1, D), jnp.float32).at[device_ids, slot_ids].add(normed_b.reshape(devices, TOK_DEV, D))
        buffers = low_back(buffers[:, :EXPERTS * CAP])
        by_expert = buffers.reshape(devices, EXPERTS, CAP, D).transpose(1, 0, 2, 3).reshape(EXPERTS, devices * CAP, D)
        results = lax.map(jax.checkpoint(expert_apply), (first_all, second_all, by_expert))
        results = results.reshape(EXPERTS, devices, CAP, D).transpose(1, 0, 2, 3).reshape(devices, EXPERTS * CAP, D)
        results = jnp.concatenate([results, jnp.zeros((devices, 1, D), jnp.float32)], axis=1)
        combined = results[device_ids, slot_ids].reshape(TOKENS, D)
        output = middle + gate[:, None] * combined
        mean_prob = lax.optimization_barrier(jnp.sum(probs * valid[:, None], axis=0)) / token_total
        balance = EXPERTS * jnp.sum(share * mean_prob)
        return (output, balance)
    primals = (tokens.astype(jnp.float32), w_qkv.astype(jnp.float32), w_out_proj.astype(jnp.float32), rel_bias, gain_attn, gain_ffn, router, w_in.astype(jnp.float32), w_out.astype(jnp.float32))
    (output, balance), pullback = jax.vjp(forward, *primals)
    grads = pullback((cotangent.astype(jnp.float32), jnp.asarray(AUX_WEIGHT, dtype=jnp.float32)))
    return (output.astype(jnp.bfloat16), grads[0], grads[1], grads[2], grads[3], grads[4], grads[5], grads[6], grads[7], grads[8], balance)
```

```python
import functools
import jax
import jax.numpy as jnp
from jax import lax
from jax.experimental import pallas as pl
from jax.experimental.pallas import tpu as pltpu
from jax.sharding import PartitionSpec as P

EPSILON = 1e-06
AUX_WEIGHT = 0.01
HIGHEST = lax.Precision.HIGHEST
MASKED = -1000000000.0
MIB = 1024 * 1024
BF16 = jnp.bfloat16
F32 = jnp.float32
LANES = 128
BLOCK = 128


def dot(left, right, contract, precision=None):
    return lax.dot_general(
        left, right, (contract, ((), ())), precision=precision, preferred_element_type=F32
    )


def nn(left, right):
    return dot(left, right, ((1,), (0,)))


def nt(left, right):
    return dot(left, right, ((1,), (1,)))


def tn(left, right):
    return dot(left, right, ((0,), (0,)))


def params(limit=56):
    return pltpu.CompilerParams(vmem_limit_bytes=limit * MIB)


def cost(flops, nbytes):
    return pl.CostEstimate(flops=int(flops), bytes_accessed=int(nbytes), transcendentals=0)


def smem():
    return pl.BlockSpec(memory_space=pltpu.SMEM)


def whole(shape):
    zeros = (0,) * len(shape)
    return pl.BlockSpec(shape, lambda *_: zeros)


def out(shape, dtype):
    return jax.ShapeDtypeStruct(shape, dtype)


def factor_of(values):
    return lax.rsqrt(jnp.mean(values * values, axis=-1, keepdims=True) + EPSILON)


def norm_back(values, factor, gain, upstream):
    weighted = upstream * gain
    cubed = factor * factor * factor
    grad = factor * weighted - values * cubed * jnp.mean(weighted * values, axis=-1, keepdims=True)
    return grad, jnp.sum(upstream * values * factor, axis=0, keepdims=True)


def valid_rows(len_ref, start, rows, seq_length, seq_count):
    index = start + lax.broadcasted_iota(jnp.int32, (rows, 1), 0)
    valid = jnp.zeros((rows, 1), jnp.bool_)
    for seq in range(seq_count):
        inside = (index >= seq * seq_length) & (index < seq * seq_length + len_ref[seq])
        valid = valid | inside
    return valid


def route_kernel(
    expert_count, capacity, len_ref, routes_ref, top_ref, left_ref, cot_ref,
    g_ref, col_ref, plain_ref, row_ref, count_ref, desc_ref, slot_row,
):
    step = pl.program_id(0)
    half = capacity // 2
    tile = g_ref.shape[0]
    rows = routes_ref.shape[1]
    length = top_ref.shape[1]
    seq_count = len_ref.shape[0]

    @pl.when(step == 0)
    def _():
        down = lax.broadcasted_iota(jnp.int32, (length, length), 0)
        along = lax.broadcasted_iota(jnp.int32, (length, length), 1)
        ahead = top_ref[...].astype(F32).T[:, 0:1]
        behind = left_ref[:, 0:1].astype(F32)
        ahead = jnp.sum(jnp.where(down == length - along, ahead, 0.0), axis=0, keepdims=True)
        behind = jnp.sum(jnp.where(down == along, behind, 0.0), axis=0, keepdims=True)
        desc_ref[:, 0:length] = ahead.astype(jnp.int32)
        desc_ref[:, length:] = behind.astype(jnp.int32)

        part = 256
        experts = lax.broadcasted_iota(jnp.int32, (LANES, part), 0)
        upper = (
            lax.broadcasted_iota(jnp.int32, (part, part), 0)
            < lax.broadcasted_iota(jnp.int32, (part, part), 1)
        )
        upper = jnp.where(upper, 1.0, 0.0).astype(BF16)
        carry = jnp.zeros((LANES, 1), F32)
        counts = jnp.zeros((8, LANES), F32)
        for start in range(0, rows, part):
            index = start + lax.broadcasted_iota(jnp.int32, (1, part), 1)
            valid = index < 0
            for seq in range(seq_count):
                first = seq * (rows // seq_count)
                valid = valid | ((index >= first) & (index < first + len_ref[seq]))
            chosen = routes_ref[:, start : start + part]
            routed = jnp.where((chosen == experts) & valid, 1.0, 0.0)
            earlier = nn(routed.astype(BF16), upper) + carry
            place = jnp.sum(earlier * routed, axis=0, keepdims=True)
            kept = valid & (place < float(capacity))
            late = place >= float(half)
            slot = chosen.astype(F32) * float(half) + place
            slot = slot + jnp.where(late, float((expert_count - 1) * half), 0.0)
            slot = jnp.where(kept, slot, -1.0)
            row_ref[:, start : start + part] = slot.astype(jnp.int32)
            turned = jnp.broadcast_to(slot, (LANES, part)).T
            col_ref[start : start + part, :] = turned[:, 0:1].astype(jnp.int32)
            slot = jnp.where(kept, chosen.astype(F32) * float(capacity) + place, -1.0)
            slot_row[:, start : start + part] = jnp.broadcast_to(slot, (8, part)).astype(jnp.int32)
            turned = jnp.broadcast_to(slot, (LANES, part)).T
            plain_ref[start : start + part, :] = turned[:, 0:1].astype(jnp.int32)
            carry = carry + jnp.sum(routed, axis=1, keepdims=True)
            counts = counts + nt(jnp.ones((8, part), BF16), routed.astype(BF16))
        count_ref[...] = counts

    slots = lax.broadcasted_iota(jnp.int32, (tile, rows), 0) + step * tile
    pick = jnp.where(slot_row[0:1, :] == slots, 1.0, 0.0).astype(BF16)
    g_ref[...] = nn(pick, cot_ref[...]).astype(BF16)


def halves(tile, width, before, steps):
    return [
        pl.BlockSpec((tile, width), lambda i: (jnp.clip(i - before, 0, steps - 1), 0)),
        pl.BlockSpec((tile, width), lambda i: (jnp.clip(i - before - steps, 0, steps - 1), 0)),
    ]


def route(seq_len, routes, buckets, cotangent, expert_count, capacity):
    rows, width = cotangent.shape
    length = buckets.shape[0]
    slots = expert_count * capacity
    tile = slots // 4
    assert tile % 16 == 0 and capacity % 2 == 0 and expert_count <= LANES
    return pl.pallas_call(
        functools.partial(route_kernel, expert_count, capacity),
        grid=(4,),
        in_specs=[
            smem(), whole((1, rows)), whole((8, length)), whole((length, LANES)), whole((rows, width)),
        ],
        out_specs=[
            pl.BlockSpec((tile, width), lambda i: (i, 0)), whole((rows, 1)), whole((rows, 1)), whole((1, rows)), whole((8, LANES)), whole((1, 2 * length)),
        ],
        out_shape=[
            out((slots, width), BF16), out((rows, 1), jnp.int32), out((rows, 1), jnp.int32),
            out((1, rows), jnp.int32), out((8, LANES), F32), out((1, 2 * length), jnp.int32),
        ],
        scratch_shapes=[pltpu.VMEM((8, rows), jnp.int32)],
        compiler_params=params(),
        cost_estimate=cost(4 * slots * rows * width, 4 * (rows + slots) * width),
        name="route",
    )(seq_len, routes, buckets, buckets, cotangent)


def qkv_kernel(scale, x_ref, gain_ref, w_ref, normed_ref, q_ref, k_ref, v_ref):
    values = x_ref[...].astype(F32)
    width = values.shape[1]
    normed = (values * factor_of(values) * gain_ref[...][None, :]).astype(BF16)
    normed_ref[...] = normed
    q_ref[...] = (nn(normed, w_ref[:, 0:width]) * scale).astype(BF16)
    k_ref[...] = nn(normed, w_ref[:, width : 2 * width]).astype(BF16)
    v_ref[...] = nn(normed, w_ref[:, 2 * width :]).astype(BF16)


def project_qkv(tokens, gain, w_qkv, scale):
    rows, width = tokens.shape
    tile = 256
    block = pl.BlockSpec((tile, width), lambda i: (i, 0))
    return pl.pallas_call(
        functools.partial(qkv_kernel, scale),
        grid=(rows // tile,),
        in_specs=[block, whole((width,)), whole((width, 3 * width))],
        out_specs=[block] * 4,
        out_shape=[out((rows, width), BF16)] * 4,
        compiler_params=params(),
        cost_estimate=cost(6 * rows * width * width, 2 * (5 * rows * width + 3 * width * width)),
        name="qkv",
    )(tokens, gain, w_qkv)


def offset_row(desc_ref, rel_ref, head):
    labels = desc_ref[...]
    row = jnp.zeros(labels.shape, F32)
    for bucket in range(rel_ref.shape[1]):
        row = row + jnp.where(labels == bucket, rel_ref[head, bucket], 0.0)
    return row


def spread(row):
    span = row.shape[1]
    spun = jnp.broadcast_to(row, (8, span))
    index = lax.broadcasted_iota(jnp.int32, (8, span), 0)
    for bit in (1, 2, 4):
        spun = jnp.where((index & bit) != 0, pltpu.roll(spun, bit, 1), spun)
    for height in (8, 16, 32, 64):
        spun = jnp.concatenate([spun, pltpu.roll(spun, height, 1)], axis=0)
    return spun


def fold(grid):
    span = grid.shape[1]
    for height in (64, 32, 16, 8):
        grid = grid[:height] + pltpu.roll(grid[height : 2 * height], span - height, 1)
    index = lax.broadcasted_iota(jnp.int32, (8, span), 0)
    for bit in (1, 2, 4):
        grid = jnp.where((index & bit) != 0, pltpu.roll(grid, span - bit, 1), grid)
    return jnp.sum(grid, axis=0, keepdims=True)


def bias_block(table, length, first, count):
    blocks = length // BLOCK
    parts = []
    for key_block in range(blocks):
        start = (blocks - key_block + first) * BLOCK
        parts.append(table[:, start : start + count * BLOCK])
    return jnp.concatenate(parts, axis=0)


def attend_kernel(head_width, len_ref, rel_ref, desc_ref, q_ref, k_ref, v_ref, o_ref, lse_ref, table_ref):
    pair = pl.program_id(0)
    seq_count = len_ref.shape[0]
    length = q_ref.shape[0] // seq_count
    per = LANES // head_width
    head_of = lax.broadcasted_iota(jnp.int32, (1, LANES), 1) // head_width
    for head in range(per):
        table_ref[head] = spread(offset_row(desc_ref, rel_ref, pair * per + head))
    items = [(seq, head) for seq in range(seq_count) for head in range(per)]

    def scores_of(seq, head):
        span = slice(seq * length, (seq + 1) * length)
        own = jnp.where(head_of == head, q_ref[span, :], jnp.zeros((), BF16))
        return nt(k_ref[span, :], own)

    ahead = scores_of(*items[0])
    mixed = []
    for index, (seq, head) in enumerate(items):
        scores = ahead
        if index + 1 < len(items):
            ahead = scores_of(*items[index + 1])
        base = seq * length
        live = lax.broadcasted_iota(jnp.int32, (length, 1), 0) < len_ref[seq]
        scores = scores + bias_block(table_ref.at[head], length, 0, length // BLOCK)
        scores = jnp.where(live, scores, MASKED)
        highest = jnp.max(scores, axis=0, keepdims=True)
        expo = jnp.exp(scores - highest)
        total = jnp.sum(expo, axis=0, keepdims=True)
        values_t = v_ref[base : base + length, :].T[head * head_width : (head + 1) * head_width]
        mixed.append(nn(values_t, expo.astype(BF16)) * (1.0 / total))
        lse_ref[0, head : head + 1, base : base + length] = highest + jnp.log(total)
        if head == per - 1:
            o_ref[base : base + length, :] = jnp.concatenate(mixed, axis=0).T.astype(BF16)
            mixed = []


def attend(seq_len, rel_bias, desc, queries, keys, values, head_width):
    rows, width = queries.shape
    per = LANES // head_width
    pairs = width // LANES
    length = rows // seq_len.shape[0]
    block = pl.BlockSpec((rows, LANES), lambda i: (0, i))
    return pl.pallas_call(
        functools.partial(attend_kernel, head_width),
        grid=(pairs,),
        in_specs=[smem(), smem(), whole(desc.shape), block, block, block],
        out_specs=[block, pl.BlockSpec((1, per, rows), lambda i: (i, 0, 0))],
        out_shape=[out((rows, width), BF16), out((pairs, per, rows), F32)],
        scratch_shapes=[pltpu.VMEM((per, BLOCK, desc.shape[1]), F32)],
        compiler_params=params(),
        cost_estimate=cost(16 * rows * length * width * 4, 8 * rows * width),
        name="attend",
    )(seq_len, rel_bias, desc, queries, keys, values)


def attend_back_kernel(
    head_width, scale, first_pair, len_ref, rel_ref, desc_ref, q_ref, k_ref, v_ref, do_ref, lse_ref,
    dq_ref, dk_ref, dv_ref, diag_ref, table_ref, sum_ref,
):
    pair = pl.program_id(0) + first_pair
    seq_count = len_ref.shape[0]
    length = q_ref.shape[0] // seq_count
    blocks = length // BLOCK
    per = LANES // head_width
    head_of = lax.broadcasted_iota(jnp.int32, (1, LANES), 1) // head_width
    for head in range(per):
        table_ref[head] = spread(offset_row(desc_ref, rel_ref, pair * per + head))
    items = [(seq, head) for seq in range(seq_count) for head in range(per)]

    def own_of(ref, seq, head):
        return jnp.where(head_of == head, ref[seq * length : (seq + 1) * length, :], jnp.zeros((), BF16))

    def products_of(seq, head):
        span = slice(seq * length, (seq + 1) * length)
        own, own_up = own_of(q_ref, seq, head), own_of(do_ref, seq, head)
        return nt(k_ref[span, :], own), nt(v_ref[span, :], own_up), own, own_up

    ahead = products_of(*items[0])
    grad_q, grad_k, grad_v = [], 0.0, 0.0
    for index, (seq, head) in enumerate(items):
        scores, weights, own, own_up = ahead
        if index + 1 < len(items):
            ahead = products_of(*items[index + 1])
        span = slice(seq * length, (seq + 1) * length)
        live = lax.broadcasted_iota(jnp.int32, (length, 1), 0) < len_ref[seq]
        scores = scores + bias_block(table_ref.at[head], length, 0, blocks)
        scores = jnp.where(live, scores, MASKED)
        probs = jnp.exp(scores - lse_ref[0, head : head + 1, span])
        product = probs * weights
        grad_s = product - probs * jnp.sum(product, axis=0, keepdims=True)
        for shift in range(1 - blocks, blocks):
            diagonal = None
            for block in range(max(0, -shift), min(blocks, blocks - shift)):
                rows = (block + shift) * BLOCK
                part = grad_s[rows : rows + BLOCK, block * BLOCK : (block + 1) * BLOCK]
                diagonal = part if diagonal is None else diagonal + part
            start = (blocks - shift) * BLOCK
            if seq == 0:
                sum_ref[head, :, start : start + BLOCK] = diagonal
            else:
                sum_ref[head, :, start : start + BLOCK] += diagonal
        grad_low = grad_s.astype(BF16)
        grad_v = grad_v + nn(probs.astype(BF16), own_up)
        grad_k = grad_k + nn(grad_low, own)
        keys_t = k_ref[span, :].T[head * head_width : (head + 1) * head_width]
        grad_q.append(nn(keys_t, grad_low))
        if head == per - 1:
            dq_ref[span, :] = (jnp.concatenate(grad_q, axis=0).T * scale).astype(BF16)
            dk_ref[span, :] = grad_k.astype(BF16)
            dv_ref[span, :] = grad_v.astype(BF16)
            grad_q, grad_k, grad_v = [], 0.0, 0.0
    for head in range(per):
        sum_ref[head, :, 0:BLOCK] = jnp.zeros((BLOCK, BLOCK), F32)
        diag_ref[0, head : head + 1, :] = fold(sum_ref[head])


def attend_back(
    seq_len, rel_bias, desc, queries, keys, values, grad_heads, lse, head_width, scale, first_pair, pairs
):
    rows = queries.shape[0]
    width = pairs * LANES
    per = LANES // head_width
    span = desc.shape[1]
    length = rows // seq_len.shape[0]
    taken = pl.BlockSpec((rows, LANES), lambda i: (0, i + first_pair))
    block = pl.BlockSpec((rows, LANES), lambda i: (0, i))
    return pl.pallas_call(
        functools.partial(attend_back_kernel, head_width, scale, first_pair),
        grid=(pairs,),
        in_specs=[
            smem(), smem(), whole(desc.shape), taken, taken, taken, taken,
            pl.BlockSpec((1, per, rows), lambda i: (i + first_pair, 0, 0)),
        ],
        out_specs=[block, block, block, pl.BlockSpec((1, per, span), lambda i: (i, 0, 0))],
        out_shape=[out((rows, width), BF16)] * 3 + [out((pairs, per, span), F32)],
        scratch_shapes=[pltpu.VMEM((per, BLOCK, span), F32)] * 2,
        compiler_params=params(),
        cost_estimate=cost(rows * length * width, rows * width),
        name="attend_back",
    )(seq_len, rel_bias, desc, queries, keys, values, grad_heads, lse)


def wide_router(router):
    first = router.astype(BF16)
    second = (router - first.astype(F32)).astype(BF16)
    rest = jnp.zeros((LANES - router.shape[0], router.shape[1]), F32)
    return [
        jnp.concatenate([part.astype(F32), rest], axis=0).astype(BF16) for part in (first, second)
    ]


def router_probs(normed, router, expert_count):
    both = nt(normed, jnp.concatenate(wide_router(router), axis=0))
    logits = both[:, :LANES] + both[:, LANES:]
    lanes = lax.broadcasted_iota(jnp.int32, logits.shape, 1)
    logits = jnp.where(lanes < expert_count, logits, -jnp.inf)
    expo = jnp.exp(logits - jnp.max(logits, axis=-1, keepdims=True))
    return expo / jnp.sum(expo, axis=-1, keepdims=True)


def middle_kernel(
    expert_count, steps, slot_tile, len_ref, attn_ref, x_ref, w_ref, gain_ref, router_ref, slot_ref,
    mid_ref, probs_ref, sums_ref, buffer_a_ref, buffer_b_ref, normed_all,
):
    step = pl.program_id(0)
    tile = attn_ref.shape[0]
    rows = slot_ref.shape[1]
    seq_count = len_ref.shape[0]

    @pl.when(step == 0)
    def _():
        sums_ref[...] = jnp.zeros_like(sums_ref)

    @pl.when(step < steps)
    def _():
        middle = x_ref[...].astype(F32) + nn(attn_ref[...], w_ref[...])
        mid_ref[...] = middle.astype(BF16)
        normed = (middle * factor_of(middle) * gain_ref[...][None, :]).astype(BF16)
        normed_all[pl.ds(pl.multiple_of(step * tile, tile), tile), :] = normed
        probs = router_probs(normed, router_ref[...], expert_count)
        probs_ref[...] = probs
        valid = valid_rows(len_ref, step * tile, tile, rows // seq_count, seq_count)
        sums_ref[...] += jnp.sum(jnp.where(valid, probs, 0.0), axis=0, keepdims=True)

    @pl.when(step >= steps)
    def _():
        slots = lax.broadcasted_iota(jnp.int32, (slot_tile, rows), 0) + (step - steps) * slot_tile
        pick = jnp.where(slot_ref[...] == slots, 1.0, 0.0).astype(BF16)
        picked = nn(pick, normed_all[...]).astype(BF16)

        @pl.when(step < steps + 2)
        def _():
            buffer_a_ref[...] = picked

        @pl.when(step >= steps + 2)
        def _():
            buffer_b_ref[...] = picked


def middle_of(seq_len, attn, tokens, w_out_proj, gain, router, slot_row, expert_count, slots):
    rows, width = attn.shape
    tile, slot_tile = 256, slots // 4
    steps = rows // tile
    block = pl.BlockSpec((tile, width), lambda i: (jnp.minimum(i, steps - 1), 0))
    return pl.pallas_call(
        functools.partial(middle_kernel, expert_count, steps, slot_tile),
        grid=(steps + 4,),
        in_specs=[
            smem(), block, block, whole((width, width)), whole((width,)), whole((expert_count, width)),
            whole((1, rows)),
        ],
        out_specs=[
            block,
            pl.BlockSpec((tile, LANES), lambda i: (jnp.minimum(i, steps - 1), 0)),
            whole((1, LANES)),
        ] + halves(slot_tile, width, steps, 2),
        out_shape=[
            out((rows, width), BF16), out((rows, LANES), F32), out((1, LANES), F32),
            out((slots // 2, width), BF16), out((slots // 2, width), BF16),
        ],
        scratch_shapes=[pltpu.VMEM((rows, width), BF16)],
        compiler_params=params(),
        cost_estimate=cost(
            2 * rows * width * (width + slots), 2 * width * (4 * rows + slots + width)
        ),
        name="middle",
    )(seq_len, attn, tokens, w_out_proj, gain, router, slot_row)


def gelu_pair(hidden):
    root = 0.7978845608028654
    square = hidden * hidden
    half = 0.5 + 0.5 * jnp.tanh(hidden * (root + (root * 0.044715) * square))
    bend = (1.0 - half) * (hidden * (2.0 * root + (6.0 * 0.044715 * root) * square))
    return hidden * half, half + half * bend


def expert_kernel(
    expert_count, me_ref, x_ref, g_ref, w_in_ref, w_out_ref, router_ref, *refs
):
    (
        result_ref, back_ref, active_ref, grad_ref, grad_rows_ref, grad_router_ref,
        result_sum, back_sum, probs_all,
    ) = refs[-9:]
    expert_step(
        expert_count, me_ref, x_ref, g_ref, w_in_ref, w_out_ref, router_ref,
        result_ref, back_ref, active_ref, grad_ref, grad_rows_ref, grad_router_ref,
        result_sum, back_sum, probs_all,
    )


def expert_step(
    expert_count, me_ref, x_ref, g_ref, w_in_ref, w_out_ref, router_ref,
    result_ref, back_ref, active_ref, grad_ref, grad_rows_ref, grad_router_ref,
    result_sum, back_sum, probs_all,
):
    step = pl.program_id(0)
    last = pl.num_programs(0) - 1
    rows = x_ref.shape[0]
    tile = rows // 2
    me = me_ref[0]
    lanes = lax.broadcasted_iota(jnp.int32, (1, LANES), 1)
    sources = g_ref.shape[0] // 2

    def cot(low):
        first = low // tile * sources
        return g_ref[first : first + sources].reshape(tile, -1).astype(F32)

    @pl.when(step == 0)
    def _():
        result_sum[...] = jnp.zeros_like(result_sum)
        back_sum[...] = jnp.zeros_like(back_sum)
        for low in range(0, rows, tile):
            probs = router_probs(x_ref[low : low + tile, :], router_ref[...], expert_count)
            probs_all[low : low + tile, :] = probs
            gate = jnp.sum(jnp.where(lanes == me, probs, 0.0), axis=1, keepdims=True)
            grad_rows_ref[low : low + tile, :] = (gate * cot(low)).astype(BF16)

    parts = [slice(low, low + tile) for low in range(0, rows, tile)]
    ahead = []
    for part in parts:
        hidden = nn(x_ref[part, :], w_in_ref[...])
        ahead.append((hidden, nt(grad_rows_ref[part, :], w_out_ref[...])))
    for part, (hidden, upstream) in zip(parts, ahead):
        active, slope = gelu_pair(hidden)
        active = active.astype(BF16)
        grad = (upstream * slope).astype(BF16)
        active_ref[part, :] = active
        grad_ref[part, :] = grad
        result_sum[part, :] += nn(active, w_out_ref[...])
        back_sum[part, :] += nt(grad, w_in_ref[...])

    @pl.when(step == last)
    def _():
        total = jnp.zeros(grad_router_ref.shape, F32)
        for low in range(0, rows, tile):
            part = slice(low, low + tile)
            result = result_sum[part, :].astype(BF16)
            first = low // tile * sources
            result_ref[first : first + sources] = result.reshape(sources, -1, result.shape[1])
            grad_gate = jnp.sum(cot(low) * result.astype(F32), axis=1, keepdims=True)
            probs = probs_all[part, :]
            own = lanes == me
            gate = jnp.sum(jnp.where(own, probs, 0.0), axis=1, keepdims=True)
            grad_logits = (grad_gate * probs * (jnp.where(own, 1.0, 0.0) - gate)).astype(BF16)
            back_ref[part, :] = (
                back_sum[part, :] + nn(grad_logits, wide_router(router_ref[...])[0])
            ).astype(BF16)
            total = total + tn(grad_logits, x_ref[part, :])[:expert_count]
        grad_router_ref[...] = total


def expert(me, received, grad_rows, w_in, w_out, router, expert_count, chunk, chunks, before):
    rows, width = received.shape
    sources, capacity = grad_rows.shape[0], grad_rows.shape[1]
    hidden = w_in.shape[1]
    tile = 512
    part = capacity // chunks
    direct = part % 16 == 0
    if not direct:
        grad_rows = grad_rows[:, chunk * part : (chunk + 1) * part]
    place = chunk if direct else 0
    piece = pl.BlockSpec((sources, part, width), lambda i: (0, place, 0))
    operands = [me, received, grad_rows, w_in, w_out, router]
    in_specs = [
        smem(), whole((rows, width)), piece,
        pl.BlockSpec((width, tile), lambda i: (0, i)),
        pl.BlockSpec((tile, width), lambda i: (i, 0)),
        whole((expert_count, width)),
    ]
    aliases = {}
    if direct and before is not None:
        aliases = {len(operands): 0}
        operands.append(before)
        in_specs.append(pl.BlockSpec(memory_space=pl.ANY))
    result, *rest = pl.pallas_call(
        functools.partial(expert_kernel, expert_count),
        grid=(hidden // tile,),
        in_specs=in_specs,
        out_specs=[
            piece, whole((rows, width)),
            pl.BlockSpec((rows, tile), lambda i: (0, i)),
            pl.BlockSpec((rows, tile), lambda i: (0, i)),
            whole((rows, width)),
            whole((expert_count, width)),
        ],
        out_shape=[
            out(grad_rows.shape, BF16), out((rows, width), BF16), out((rows, hidden), BF16),
            out((rows, hidden), BF16), out((rows, width), BF16), out((expert_count, width), F32),
        ],
        scratch_shapes=[
            pltpu.VMEM((rows, width), F32), pltpu.VMEM((rows, width), F32),
            pltpu.VMEM((rows, LANES), F32),
        ],
        input_output_aliases=aliases,
        compiler_params=params(),
        cost_estimate=cost(16 * rows * width * hidden, 4 * rows * (hidden + 2 * width)),
        name="expert",
    )(*operands)
    if not direct and before is not None:
        result = jnp.concatenate([before, result], axis=1)
    return result, *rest


def grad_w_out_kernel(active_a_ref, active_b_ref, g_a_ref, g_b_ref, out_ref):
    grad = tn(active_a_ref[...], g_a_ref[...]) + tn(active_b_ref[...], g_b_ref[...])
    out_ref[...] = grad.astype(BF16)


def grad_w_in_kernel(grad_a_ref, grad_b_ref, x_a_ref, x_b_ref, out_ref, turned):
    rows = x_a_ref.shape[0]

    @pl.when(pl.program_id(0) == 0)
    def _():
        turned[:, 0:rows] = x_a_ref[...].T
        turned[:, rows:] = x_b_ref[...].T

    grad = nn(turned[:, 0:rows], grad_a_ref[...]) + nn(turned[:, rows:], grad_b_ref[...])
    out_ref[...] = grad.astype(BF16)


def grad_of_expert(kernel, moving, still, shares, turned, name):
    rows, width = still[0].shape
    hidden = moving[0].shape[1]
    part = hidden // shares
    shape = (width, part) if turned else (part, width)
    block = pl.BlockSpec((rows, part), lambda i: (0, i))
    return pl.pallas_call(
        kernel,
        grid=(shares,),
        in_specs=[block] * 2 + [whole((rows, width))] * 2,
        out_specs=pl.BlockSpec((None, *shape), lambda i: (i, 0, 0)),
        out_shape=out((shares, *shape), BF16),
        scratch_shapes=[pltpu.VMEM((width, 2 * rows), BF16)] * turned,
        compiler_params=params(),
        cost_estimate=cost(8 * rows * width * hidden, 2 * (2 * rows + width) * (hidden + width)),
        name=name,
    )(*moving, *still)


def gather_rows(slot_ref, tile, *refs):
    rows = refs[0].shape[0]
    total = None
    for index, ref in enumerate(refs):
        slots = lax.broadcasted_iota(jnp.int32, (tile, rows), 1) + index * rows
        pick = jnp.where(slot_ref[...] == slots, 1.0, 0.0).astype(BF16)
        more = nn(pick, ref[...])
        total = more if total is None else total + more
    return total


def combine_back_kernel(
    balance_scale, expert_count, len_ref, back_a_ref, back_b_ref, slot_ref, cot_ref, mid_ref, probs_ref,
    w_ref, router_ref, gain_ref, counts_ref, rows_total,
    branch_ref, heads_ref, grad_gain_ref, grad_router_ref,
):
    step = pl.program_id(0)
    tile = mid_ref.shape[0]
    seq_count = len_ref.shape[0]
    probs = probs_ref[...]
    valid = valid_rows(len_ref, step * tile, tile, rows_total // seq_count, seq_count)
    pull = jnp.where(valid, counts_ref[0:1, :] * balance_scale, 0.0)
    grad_logits = (probs * (pull - jnp.sum(probs * pull, axis=1, keepdims=True))).astype(BF16)
    grad_normed = gather_rows(slot_ref, tile, back_a_ref, back_b_ref)
    grad_normed = grad_normed + nn(grad_logits, wide_router(router_ref[...])[0])
    middle = mid_ref[...].astype(F32)
    factor = factor_of(middle)
    gain = gain_ref[...][None, :]
    normed = (middle * factor * gain).astype(BF16)
    grad_mid, grad_gain = norm_back(middle, factor, gain, grad_normed)
    grad_mid = grad_mid + cot_ref[...].astype(F32)
    branch = grad_mid.astype(BF16)
    branch_ref[...] = branch
    heads_ref[...] = nt(branch, w_ref[...]).astype(BF16)
    grad_router = tn(grad_logits, normed)[:expert_count]

    @pl.when(step == 0)
    def _():
        grad_gain_ref[...] = grad_gain
        grad_router_ref[...] = grad_router

    @pl.when(step > 0)
    def _():
        grad_gain_ref[...] += grad_gain
        grad_router_ref[...] += grad_router


def combine_back(
    seq_len, back, slot_col, cotangent, middle, probs, w_out_proj, router, gain, counts, balance_scale
):
    rows, width = middle.shape
    slots = 2 * back[0].shape[0]
    expert_count = router.shape[0]
    tile = 256
    block = pl.BlockSpec((tile, width), lambda i: (i, 0))

    def kernel(*refs):
        combine_back_kernel(balance_scale, expert_count, *refs[:11], rows, *refs[11:])

    return pl.pallas_call(
        kernel,
        grid=(rows // tile,),
        in_specs=[
            smem(), whole((slots // 2, width)), whole((slots // 2, width)),
            pl.BlockSpec((tile, 1), lambda i: (i, 0)), block, block,
            pl.BlockSpec((tile, LANES), lambda i: (i, 0)), whole((width, width)),
            whole((expert_count, width)), whole((width,)), whole((8, LANES)),
        ],
        out_specs=[block, block, whole((1, width)), whole((expert_count, width))],
        out_shape=[
            out((rows, width), BF16), out((rows, width), BF16),
            out((1, width), F32), out((expert_count, width), F32),
        ],
        compiler_params=params(),
        cost_estimate=cost(
            rows * width, rows * width
        ),
        name="combine_back",
    )(seq_len, *back, slot_col, cotangent, middle, probs, w_out_proj, router, gain, counts)


def output_kernel(expert_count, back_ref, slot_ref, mid_ref, probs_ref, out_ref):
    tile = mid_ref.shape[0]
    capacity = back_ref.shape[0] // expert_count
    combined = gather_rows(slot_ref, tile, back_ref)
    first = lax.broadcasted_iota(jnp.int32, (tile, LANES), 1) * capacity
    slot = slot_ref[...]
    own = (slot >= first) & (slot < first + capacity)
    gate = jnp.sum(jnp.where(own, probs_ref[...], 0.0), axis=1, keepdims=True)
    out_ref[...] = (mid_ref[...].astype(F32) + gate * combined).astype(BF16)


def layer_output(returned, slot_col, middle, probs, expert_count):
    rows, width = middle.shape
    slots = returned.shape[0]
    tile = 256
    block = pl.BlockSpec((tile, width), lambda i: (i, 0))
    thin = pl.BlockSpec((tile, 1), lambda i: (i, 0))
    return pl.pallas_call(
        functools.partial(output_kernel, expert_count),
        grid=(rows // tile,),
        in_specs=[
            whole((slots, width)), thin, block, pl.BlockSpec((tile, LANES), lambda i: (i, 0)),
        ],
        out_specs=block,
        out_shape=out((rows, width), BF16),
        compiler_params=params(),
        cost_estimate=cost(2 * rows * width * slots, 2 * width * (3 * rows + slots)),
        name="layer_output",
    )(returned, slot_col, middle, probs)


def grad_weights_kernel(counts, core_ref, *refs):
    lefts, refs = refs[: len(counts)], refs[len(counts) :]
    rights, refs = refs[: sum(counts)], refs[sum(counts) :]
    (keep_ref, send_ref), turned = refs[:2], refs[2:]
    half, tile = keep_ref.shape[1], keep_ref.shape[2]

    @pl.when(pl.program_id(0) == 0)
    def _():
        for left, scratch in zip(lefts, turned):
            scratch[...] = left[...].T

    for index, result in enumerate((keep_ref, send_ref)):
        side = core_ref[0] if index == 0 else 1 - core_ref[0]
        done = 0
        for count, scratch in zip(counts, turned):
            left = scratch[pl.ds(pl.multiple_of(side * half, half), half), :]
            right = jnp.concatenate([ref[...] for ref in rights[done : done + count]], axis=1)
            product = nn(left, right).astype(BF16)
            for place in range(count):
                result[done + place] = product[:, place * tile : (place + 1) * tile]
            done += count


def grad_of_weights(core, pairs, span):
    rows, width = pairs[0][0].shape
    counts = tuple(len(rights) for _, rights in pairs)
    tile = 128
    result = pl.BlockSpec((sum(counts), width // 2, tile), lambda i: (0, 0, i))
    lefts = [left for left, _ in pairs]
    rights = [right for _, some in pairs for right in some]
    total = out((sum(counts), width // 2, span), BF16)
    return pl.pallas_call(
        functools.partial(grad_weights_kernel, counts),
        grid=(span // tile,),
        in_specs=[smem()] + [whole((rows, width))] * len(lefts) + [
            pl.BlockSpec((rows, tile), lambda i, first=first // tile: (0, i + first)) for _, first in rights
        ],
        out_specs=[result, result],
        out_shape=[total, total],
        scratch_shapes=[pltpu.VMEM((width, rows), BF16)] * len(lefts),
        compiler_params=params(),
        cost_estimate=cost(
            rows * width, rows * width
        ),
        name="grad_weights",
    )(core, *lefts, *[right for right, _ in rights])


def add_split_kernel(me_ref, keep_ref, got_ref, *outs):
    total = (keep_ref[...].astype(F32) + got_ref[...].astype(F32)).astype(BF16)
    for index, ref in enumerate(outs):

        @pl.when(pl.program_id(0) == index)
        def _(ref=ref):
            ref[...] = total


def add_split(me, keep, got, shares):
    rows, span = keep.shape
    piece = rows // shares
    block = pl.BlockSpec((None, piece, span), lambda i, me: (me[0] ^ i, 0, 0))
    return pl.pallas_call(
        add_split_kernel,
        grid_spec=pltpu.PrefetchScalarGridSpec(
            num_scalar_prefetch=1,
            grid=(shares,),
            in_specs=[block, block],
            out_specs=[whole((piece, span))] * shares,
        ),
        out_shape=[out((piece, span), BF16)] * shares,
        compiler_params=params(),
        cost_estimate=cost(rows * span, 8 * rows * span),
        name="add_split",
    )(me, keep.reshape(shares, piece, span), got.reshape(shares, piece, span))


def grad_tokens_kernel(groups, *refs):
    grad_refs, (w_ref, x_ref, gain_ref, mid_ref, out_ref, grad_gain_ref) = refs[: 3 * groups], refs[3 * groups :]
    step = pl.program_id(0)
    width = x_ref.shape[1]
    span = width // groups
    upstream = 0.0
    for group in range(groups):
        for part in range(3):
            start = part * width + group * span
            upstream = upstream + nt(grad_refs[3 * group + part][...], w_ref[:, start : start + span])
    values = x_ref[...].astype(F32)
    grad, grad_gain = norm_back(values, factor_of(values), gain_ref[...][None, :], upstream)
    out_ref[...] = mid_ref[...].astype(F32) + grad

    @pl.when(step == 0)
    def _():
        grad_gain_ref[...] = grad_gain

    @pl.when(step > 0)
    def _():
        grad_gain_ref[...] += grad_gain


def grad_of_tokens(grads, w_qkv, tokens, gain, grad_mid):
    rows, width = tokens.shape
    groups = len(grads) // 3
    tile = 256
    block = pl.BlockSpec((tile, width), lambda i: (i, 0))
    taken = pl.BlockSpec((tile, width // groups), lambda i: (i, 0))
    return pl.pallas_call(
        functools.partial(grad_tokens_kernel, groups),
        grid=(rows // tile,),
        in_specs=[taken] * len(grads) + [whole((width, 3 * width)), block, whole((width,)), block],
        out_specs=[block, whole((1, width))],
        out_shape=[out((rows, width), F32), out((1, width), F32)],
        compiler_params=params(),
        cost_estimate=cost(rows * width, rows * width),
        name="grad_tokens",
    )(*grads, w_qkv, tokens, gain, grad_mid)


def after(value, *earlier):
    return lax.optimization_barrier((value, *earlier))[0]


def swap(value, axis, mask):
    return lax.ppermute(value, axis, [(i, i ^ mask) for i in range(lax.axis_size(axis))])


def tree(parts):
    parts = [part.astype(F32) for part in parts]
    while len(parts) > 1:
        parts = [parts[i] + parts[i + 1] for i in range(0, len(parts), 2)]
    return parts[0]


class Group:
    def __init__(self, axis, shift, size):
        self.axis, self.shift, self.size = axis, shift, size
        self.index = (lax.axis_index(axis) >> shift) % size

    def swaps(self, of):
        return [swap(of(d), self.axis, d << self.shift) for d in range(1, self.size)]

    def total(self, value):
        return tree([value] + self.swaps(lambda d: value))

    def doubled(self, value, bit):
        while bit < self.size:
            value = tree([value, swap(value, self.axis, bit << self.shift)]).astype(value.dtype)
            bit *= 2
        return value

    def parts(self, pieces):
        return [pieces[0]] + self.swaps(lambda d: pieces[d])

    def gather(self, value):
        parts = [value] + self.swaps(lambda d: value)
        bit = 1
        while bit < self.size:
            flip = (self.index & bit) != 0
            parts = [jnp.where(flip, parts[j ^ bit], parts[j]) for j in range(self.size)]
            bit *= 2
        return jnp.stack(parts)


def gather_pieces(piece, shape, core, data):
    return core.gather(data.gather(piece).reshape(shape))


def body(
    tokens,
    cotangent,
    routes,
    seq_len,
    buckets,
    w_qkv,
    w_out_proj,
    rel_bias,
    gain_attn,
    gain_ffn,
    router,
    w_in,
    w_out,
):
    rows, width = tokens.shape
    bucket_count, heads_count = rel_bias.shape
    head_width = width // heads_count
    expert_count = router.shape[1]
    capacity = max(2, (5 * rows + 4 * expert_count - 1) // (4 * expert_count))
    slots = expert_count * capacity
    shares, experts_axis = lax.axis_size("dp"), lax.axis_size("expert")
    token_total = float(rows * shares * experts_axis)
    scale = head_width ** (-0.5)
    first_mat, second_mat = w_in[0], w_out[0]
    router_t, rel_t = router.T, rel_bias.T
    me = lax.axis_index("expert").astype(jnp.int32)[None]
    me_dp = lax.axis_index("dp").astype(jnp.int32)[None]
    core = Group("expert", 0, 2)
    line = Group("expert", 1, experts_axis // 2)
    data = Group("dp", 0, shares)

    def exchange(array):
        return lax.all_to_all(array, "expert", split_axis=0, concat_axis=0, tiled=True)

    def sum_small(array):
        return line.total(data.total(core.total(array)))

    grad_rows, slot_col, slot_plain, slot_row, counts, desc = route(
        seq_len, routes.T, buckets, cotangent, expert_count, capacity
    )
    grad_rows = exchange(grad_rows)
    counts = sum_small(counts)

    normed_a, queries, keys, values = project_qkv(tokens, gain_attn, w_qkv, scale)
    attn, lse = attend(seq_len, rel_t, desc, queries, keys, values, head_width)
    middle, probs, prob_sums, *buffer = middle_of(
        seq_len, attn, tokens, w_out_proj, gain_ffn, router_t, slot_row, expert_count, slots
    )
    buffer[0], buffer[1], grad_rows = lax.optimization_barrier((*buffer, grad_rows))
    received = [exchange(part) for part in buffer]
    received[0], counts = lax.optimization_barrier((received[0], counts))
    grad_rows = grad_rows.reshape(experts_axis, -1, width)
    result, done = None, []
    for chunk in range(2):
        result, *rest = expert(
            me, received[chunk], grad_rows, first_mat, second_mat, router_t, expert_count, chunk, 2, result
        )
        done.append(rest)
    back, active, grad_hidden, grad_result, grad_router_e = zip(*done)
    first_back = exchange(back[0])
    back = [first_back, exchange(after(back[1], first_back))]

    def scatter_shares(grad):
        return lax.psum_scatter(grad, "dp", scatter_dimension=0, tiled=True)

    active, back[0] = lax.optimization_barrier((active, back[0]))
    grad_second = grad_of_expert(grad_w_out_kernel, active, grad_result, shares, 0, "grad_w_out")
    grad_hidden, grad_second = lax.optimization_barrier((grad_hidden, grad_second))
    grad_first = grad_of_expert(grad_w_in_kernel, grad_hidden, received, shares, 1, "grad_w_in")
    back[1], grad_first = lax.optimization_barrier((back[1], grad_first))
    grad_second = scatter_shares(grad_second)
    grad_first = scatter_shares(grad_first)

    branch, grad_heads, grad_gain_b, grad_router_t = combine_back(
        seq_len, back, slot_col, cotangent, middle, probs, w_out_proj, router_t, gain_ffn, counts,
        AUX_WEIGHT * expert_count / token_total / token_total,
    )
    returned = exchange(after(result.reshape(slots, width), grad_heads))
    grad_router = grad_router_e[0] + grad_router_e[1] + grad_router_t
    core_index = me & 1

    groups = 2
    pairs = width // LANES // groups
    span = pairs * LANES
    grads, diags, sums = [], [], []
    for group in range(groups):
        *some, diag = attend_back(
            seq_len, rel_t, desc, queries, keys, values, grad_heads, lse, head_width, scale,
            group * pairs, pairs,
        )
        grads += some
        diags.append(diag.reshape(heads_count // groups, -1))
        products = [(normed_a, [(part, 0) for part in some])]
        if group == 1:
            some, got, grad_second = lax.optimization_barrier((some, got, grad_second))
            pieces = add_split(me_dp, keep.reshape(-1, span), got.reshape(-1, span), shares)
            *some, own = lax.optimization_barrier((*some, pieces[0]))
            pieces = [own, *pieces[1:]]
            products = [(normed_a, [(part, 0) for part in some])]
        if group == 0:
            products.append((attn, [(branch, first) for first in range(0, width, span)]))
            keep, send = grad_of_weights(core_index, products, span)
            got = swap(send, "expert", 1)
            grad_heads, keep = lax.optimization_barrier((grad_heads, keep))
            shape = keep.shape
        else:
            keep, send = grad_of_weights(core_index, products, span)
            got = swap(send, "expert", 1)
            parts = data.parts(pieces)
            grads, keep, returned = lax.optimization_barrier((grads, keep, returned))
            grad_tokens, grad_gain_a = grad_of_tokens(grads, w_qkv, tokens, gain_attn, branch)
            grad_tokens, parts, got, grad_first = lax.optimization_barrier((grad_tokens, parts, got, grad_first))
            piece = tree(parts).astype(BF16)
            moved = swap(piece, line.axis, 2)
            pieces = add_split(me_dp, keep.reshape(-1, span), got.reshape(-1, span), shares)
            onehot = (desc == jnp.arange(bucket_count, dtype=jnp.int32)[:, None]).astype(F32)
            grad_rel = dot(onehot, jnp.concatenate(diags, axis=0), ((1,), (1,)), HIGHEST)
            small = [grad_gain_a, grad_gain_b, grad_router, prob_sums, grad_rel]
            packed = jnp.concatenate([part.reshape(-1) for part in small]).reshape(-1, LANES)
            packed = core.total(packed)
            returned, own, packed = lax.optimization_barrier((returned, pieces[0], packed))
            packed = data.parts([packed] * shares)
            parts = data.parts([own, *pieces[1:]])
            output = layer_output(returned, slot_plain, middle, probs, expert_count)
            grad_first, grad_second = grad_first.astype(F32), grad_second.astype(F32)
            output, moved, parts, packed, grad_first, grad_second = lax.optimization_barrier(
                (output, moved, parts, packed, grad_first, grad_second)
            )
            piece = line.doubled(tree([piece, moved]).astype(BF16), 2)
            sums.append(gather_pieces(piece, shape, core, data))
            piece = line.doubled(tree(parts).astype(BF16), 1)
            packed = line.parts([tree(packed)] * line.size)
            piece, packed = lax.optimization_barrier((piece, packed))
            sums.append(gather_pieces(piece, keep.shape, core, data))

    packed = tree(packed)
    packed, summed = packed.reshape(-1), []
    for part in small:
        summed.append(packed[: part.size].reshape(part.shape))
        packed = packed[part.size :]
    balance = expert_count * jnp.sum((counts[0] / token_total) * (summed[3][0] / token_total))

    def both_halves(columns):
        rows_of = [jnp.concatenate([part[half, i] for part, i in columns], axis=1) for half in range(2)]
        return jnp.concatenate(rows_of, axis=0).astype(F32)

    grad_qkv = both_halves([(sums[g], i) for i in range(3) for g in range(groups)])
    grad_proj = both_halves([(sums[0], 3 + g) for g in range(groups)])
    return (
        output,
        grad_tokens,
        grad_qkv,
        grad_proj,
        summed[4],
        summed[0][0],
        summed[1][0],
        summed[2].T,
        grad_first,
        grad_second,
        balance,
    )


def solution(mesh):
    placed = (
        P(("dp", "expert"), None),
        P(("dp", "expert"), None),
        P(("dp", "expert"), None),
        P(("dp", "expert")),
        P(),
        P(),
        P(),
        P(),
        P(),
        P(),
        P(),
        P("expert", None, None),
        P("expert", None, None),
    )
    return jax.shard_map(
        body,
        mesh=mesh,
        in_specs=placed,
        out_specs=(
            P(("dp", "expert"), None),
            P(("dp", "expert"), None),
            P(),
            P(),
            P(),
            P(),
            P(),
            P(),
            P("expert", None, "dp"),
            P("expert", "dp", None),
            P(),
        ),
        check_vma=False,
    )
```

```python
import functools
import jax
import jax.numpy as jnp
from jax import lax
from jax.experimental import pallas as pl
from jax.experimental.pallas import tpu as pltpu
from jax.sharding import PartitionSpec as P

EPSILON = 1e-06
AUX_WEIGHT = 0.01
HIGHEST = lax.Precision.HIGHEST
MASKED = -1000000000.0
MIB = 1024 * 1024
BF16 = jnp.bfloat16
F32 = jnp.float32
LANES = 128
BLOCK = 128


def dot(left, right, contract, precision=None):
    return lax.dot_general(
        left, right, (contract, ((), ())), precision=precision, preferred_element_type=F32
    )


def nn(left, right):
    return dot(left, right, ((1,), (0,)))


def nt(left, right):
    return dot(left, right, ((1,), (1,)))


def tn(left, right):
    return dot(left, right, ((0,), (0,)))


def params(limit=56):
    return pltpu.CompilerParams(vmem_limit_bytes=limit * MIB)


def cost(flops, nbytes):
    return pl.CostEstimate(flops=int(flops), bytes_accessed=int(nbytes), transcendentals=0)


def smem():
    return pl.BlockSpec(memory_space=pltpu.SMEM)


def whole(shape):
    zeros = (0,) * len(shape)
    return pl.BlockSpec(shape, lambda *_: zeros)


def out(shape, dtype):
    return jax.ShapeDtypeStruct(shape, dtype)


def factor_of(values):
    return lax.rsqrt(jnp.mean(values * values, axis=-1, keepdims=True) + EPSILON)


def norm_back(values, factor, gain, upstream):
    weighted = upstream * gain
    cubed = factor * factor * factor
    grad = factor * weighted - values * cubed * jnp.mean(weighted * values, axis=-1, keepdims=True)
    return grad, jnp.sum(upstream * values * factor, axis=0, keepdims=True)


def valid_rows(len_ref, start, rows, seq_length, seq_count):
    index = start + lax.broadcasted_iota(jnp.int32, (rows, 1), 0)
    valid = jnp.zeros((rows, 1), jnp.bool_)
    for seq in range(seq_count):
        inside = (index >= seq * seq_length) & (index < seq * seq_length + len_ref[seq])
        valid = valid | inside
    return valid


def route_kernel(
    expert_count, capacity, len_ref, routes_ref, top_ref, left_ref, cot_ref,
    g_ref, col_ref, plain_ref, row_ref, count_ref, desc_ref, slot_row,
):
    step = pl.program_id(0)
    half = capacity // 2
    tile = g_ref.shape[0]
    rows = routes_ref.shape[1]
    length = top_ref.shape[1]
    seq_count = len_ref.shape[0]

    @pl.when(step == 0)
    def _():
        down = lax.broadcasted_iota(jnp.int32, (length, length), 0)
        along = lax.broadcasted_iota(jnp.int32, (length, length), 1)
        ahead = top_ref[...].astype(F32).T[:, 0:1]
        behind = left_ref[:, 0:1].astype(F32)
        ahead = jnp.sum(jnp.where(down == length - along, ahead, 0.0), axis=0, keepdims=True)
        behind = jnp.sum(jnp.where(down == along, behind, 0.0), axis=0, keepdims=True)
        desc_ref[:, 0:length] = ahead.astype(jnp.int32)
        desc_ref[:, length:] = behind.astype(jnp.int32)

        part = 256
        experts = lax.broadcasted_iota(jnp.int32, (LANES, part), 0)
        upper = (
            lax.broadcasted_iota(jnp.int32, (part, part), 0)
            < lax.broadcasted_iota(jnp.int32, (part, part), 1)
        )
        upper = jnp.where(upper, 1.0, 0.0).astype(BF16)
        carry = jnp.zeros((LANES, 1), F32)
        counts = jnp.zeros((8, LANES), F32)
        for start in range(0, rows, part):
            index = start + lax.broadcasted_iota(jnp.int32, (1, part), 1)
            valid = index < 0
            for seq in range(seq_count):
                first = seq * (rows // seq_count)
                valid = valid | ((index >= first) & (index < first + len_ref[seq]))
            chosen = routes_ref[:, start : start + part]
            routed = jnp.where((chosen == experts) & valid, 1.0, 0.0)
            earlier = nn(routed.astype(BF16), upper) + carry
            place = jnp.sum(earlier * routed, axis=0, keepdims=True)
            kept = valid & (place < float(capacity))
            late = place >= float(half)
            slot = chosen.astype(F32) * float(half) + place
            slot = slot + jnp.where(late, float((expert_count - 1) * half), 0.0)
            slot = jnp.where(kept, slot, -1.0)
            row_ref[:, start : start + part] = slot.astype(jnp.int32)
            turned = jnp.broadcast_to(slot, (LANES, part)).T
            col_ref[start : start + part, :] = turned[:, 0:1].astype(jnp.int32)
            slot = jnp.where(kept, chosen.astype(F32) * float(capacity) + place, -1.0)
            slot_row[:, start : start + part] = jnp.broadcast_to(slot, (8, part)).astype(jnp.int32)
            turned = jnp.broadcast_to(slot, (LANES, part)).T
            plain_ref[start : start + part, :] = turned[:, 0:1].astype(jnp.int32)
            carry = carry + jnp.sum(routed, axis=1, keepdims=True)
            counts = counts + nt(jnp.ones((8, part), BF16), routed.astype(BF16))
        count_ref[...] = counts

    slots = lax.broadcasted_iota(jnp.int32, (tile, rows), 0) + step * tile
    pick = jnp.where(slot_row[0:1, :] == slots, 1.0, 0.0).astype(BF16)
    g_ref[...] = nn(pick, cot_ref[...]).astype(BF16)


def halves(tile, width, before, steps):
    return [
        pl.BlockSpec((tile, width), lambda i: (jnp.clip(i - before, 0, steps - 1), 0)),
        pl.BlockSpec((tile, width), lambda i: (jnp.clip(i - before - steps, 0, steps - 1), 0)),
    ]


def route(seq_len, routes, buckets, cotangent, expert_count, capacity):
    rows, width = cotangent.shape
    length = buckets.shape[0]
    slots = expert_count * capacity
    tile = slots // 4
    assert tile % 16 == 0 and capacity % 2 == 0 and expert_count <= LANES
    return pl.pallas_call(
        functools.partial(route_kernel, expert_count, capacity),
        grid=(4,),
        in_specs=[
            smem(), whole((1, rows)), whole((8, length)), whole((length, LANES)), whole((rows, width)),
        ],
        out_specs=[
            pl.BlockSpec((tile, width), lambda i: (i, 0)), whole((rows, 1)), whole((rows, 1)), whole((1, rows)), whole((8, LANES)), whole((1, 2 * length)),
        ],
        out_shape=[
            out((slots, width), BF16), out((rows, 1), jnp.int32), out((rows, 1), jnp.int32),
            out((1, rows), jnp.int32), out((8, LANES), F32), out((1, 2 * length), jnp.int32),
        ],
        scratch_shapes=[pltpu.VMEM((8, rows), jnp.int32)],
        compiler_params=params(),
        cost_estimate=cost(4 * slots * rows * width, 4 * (rows + slots) * width),
        name="route",
    )(seq_len, routes, buckets, buckets, cotangent)


def qkv_kernel(scale, x_ref, gain_ref, w_ref, normed_ref, q_ref, k_ref, v_ref):
    values = x_ref[...].astype(F32)
    width = values.shape[1]
    normed = (values * factor_of(values) * gain_ref[...][None, :]).astype(BF16)
    normed_ref[...] = normed
    q_ref[...] = (nn(normed, w_ref[:, 0:width]) * scale).astype(BF16)
    k_ref[...] = nn(normed, w_ref[:, width : 2 * width]).astype(BF16)
    v_ref[...] = nn(normed, w_ref[:, 2 * width :]).astype(BF16)


def project_qkv(tokens, gain, w_qkv, scale):
    rows, width = tokens.shape
    tile = 256
    block = pl.BlockSpec((tile, width), lambda i: (i, 0))
    return pl.pallas_call(
        functools.partial(qkv_kernel, scale),
        grid=(rows // tile,),
        in_specs=[block, whole((width,)), whole((width, 3 * width))],
        out_specs=[block] * 4,
        out_shape=[out((rows, width), BF16)] * 4,
        compiler_params=params(),
        cost_estimate=cost(6 * rows * width * width, 2 * (5 * rows * width + 3 * width * width)),
        name="qkv",
    )(tokens, gain, w_qkv)


def offset_row(desc_ref, rel_ref, head):
    labels = desc_ref[...]
    row = jnp.zeros(labels.shape, F32)
    for bucket in range(rel_ref.shape[1]):
        row = row + jnp.where(labels == bucket, rel_ref[head, bucket], 0.0)
    return row


def spread(row):
    span = row.shape[1]
    spun = jnp.broadcast_to(row, (8, span))
    index = lax.broadcasted_iota(jnp.int32, (8, span), 0)
    for bit in (1, 2, 4):
        spun = jnp.where((index & bit) != 0, pltpu.roll(spun, bit, 1), spun)
    for height in (8, 16, 32, 64):
        spun = jnp.concatenate([spun, pltpu.roll(spun, height, 1)], axis=0)
    return spun


def fold(grid):
    span = grid.shape[1]
    for height in (64, 32, 16, 8):
        grid = grid[:height] + pltpu.roll(grid[height : 2 * height], span - height, 1)
    index = lax.broadcasted_iota(jnp.int32, (8, span), 0)
    for bit in (1, 2, 4):
        grid = jnp.where((index & bit) != 0, pltpu.roll(grid, span - bit, 1), grid)
    return jnp.sum(grid, axis=0, keepdims=True)


def bias_block(table, length, first, count):
    blocks = length // BLOCK
    parts = []
    for key_block in range(blocks):
        start = (blocks - key_block + first) * BLOCK
        parts.append(table[:, start : start + count * BLOCK])
    return jnp.concatenate(parts, axis=0)


def attend_kernel(head_width, len_ref, rel_ref, desc_ref, q_ref, k_ref, v_ref, o_ref, lse_ref, table_ref):
    pair = pl.program_id(0)
    seq_count = len_ref.shape[0]
    length = q_ref.shape[0] // seq_count
    per = LANES // head_width
    head_of = lax.broadcasted_iota(jnp.int32, (1, LANES), 1) // head_width
    for head in range(per):
        table_ref[head] = spread(offset_row(desc_ref, rel_ref, pair * per + head))
    items = [(seq, head) for seq in range(seq_count) for head in range(per)]

    def scores_of(seq, head):
        span = slice(seq * length, (seq + 1) * length)
        own = jnp.where(head_of == head, q_ref[span, :], jnp.zeros((), BF16))
        return nt(k_ref[span, :], own)

    ahead = scores_of(*items[0])
    mixed = []
    for index, (seq, head) in enumerate(items):
        scores = ahead
        if index + 1 < len(items):
            ahead = scores_of(*items[index + 1])
        base = seq * length
        live = lax.broadcasted_iota(jnp.int32, (length, 1), 0) < len_ref[seq]
        scores = scores + bias_block(table_ref.at[head], length, 0, length // BLOCK)
        scores = jnp.where(live, scores, MASKED)
        highest = jnp.max(scores, axis=0, keepdims=True)
        expo = jnp.exp(scores - highest)
        total = jnp.sum(expo, axis=0, keepdims=True)
        values_t = v_ref[base : base + length, :].T[head * head_width : (head + 1) * head_width]
        mixed.append(nn(values_t, expo.astype(BF16)) * (1.0 / total))
        lse_ref[0, head : head + 1, base : base + length] = highest + jnp.log(total)
        if head == per - 1:
            o_ref[base : base + length, :] = jnp.concatenate(mixed, axis=0).T.astype(BF16)
            mixed = []


def attend(seq_len, rel_bias, desc, queries, keys, values, head_width):
    rows, width = queries.shape
    per = LANES // head_width
    pairs = width // LANES
    length = rows // seq_len.shape[0]
    block = pl.BlockSpec((rows, LANES), lambda i: (0, i))
    return pl.pallas_call(
        functools.partial(attend_kernel, head_width),
        grid=(pairs,),
        in_specs=[smem(), smem(), whole(desc.shape), block, block, block],
        out_specs=[block, pl.BlockSpec((1, per, rows), lambda i: (i, 0, 0))],
        out_shape=[out((rows, width), BF16), out((pairs, per, rows), F32)],
        scratch_shapes=[pltpu.VMEM((per, BLOCK, desc.shape[1]), F32)],
        compiler_params=params(),
        cost_estimate=cost(16 * rows * length * width * 4, 8 * rows * width),
        name="attend",
    )(seq_len, rel_bias, desc, queries, keys, values)


def attend_back_kernel(
    head_width, scale, first_pair, len_ref, rel_ref, desc_ref, q_ref, k_ref, v_ref, do_ref, lse_ref,
    dq_ref, dk_ref, dv_ref, diag_ref, table_ref, sum_ref,
):
    pair = pl.program_id(0) + first_pair
    seq_count = len_ref.shape[0]
    length = q_ref.shape[0] // seq_count
    blocks = length // BLOCK
    per = LANES // head_width
    head_of = lax.broadcasted_iota(jnp.int32, (1, LANES), 1) // head_width
    for head in range(per):
        table_ref[head] = spread(offset_row(desc_ref, rel_ref, pair * per + head))
    items = [(seq, head) for seq in range(seq_count) for head in range(per)]

    def own_of(ref, seq, head):
        return jnp.where(head_of == head, ref[seq * length : (seq + 1) * length, :], jnp.zeros((), BF16))

    def products_of(seq, head):
        span = slice(seq * length, (seq + 1) * length)
        own, own_up = own_of(q_ref, seq, head), own_of(do_ref, seq, head)
        return nt(k_ref[span, :], own), nt(v_ref[span, :], own_up), own, own_up

    ahead = products_of(*items[0])
    grad_q, grad_k, grad_v = [], 0.0, 0.0
    for index, (seq, head) in enumerate(items):
        scores, weights, own, own_up = ahead
        if index + 1 < len(items):
            ahead = products_of(*items[index + 1])
        span = slice(seq * length, (seq + 1) * length)
        live = lax.broadcasted_iota(jnp.int32, (length, 1), 0) < len_ref[seq]
        scores = scores + bias_block(table_ref.at[head], length, 0, blocks)
        scores = jnp.where(live, scores, MASKED)
        probs = jnp.exp(scores - lse_ref[0, head : head + 1, span])
        product = probs * weights
        grad_s = product - probs * jnp.sum(product, axis=0, keepdims=True)
        for shift in range(1 - blocks, blocks):
            diagonal = None
            for block in range(max(0, -shift), min(blocks, blocks - shift)):
                rows = (block + shift) * BLOCK
                part = grad_s[rows : rows + BLOCK, block * BLOCK : (block + 1) * BLOCK]
                diagonal = part if diagonal is None else diagonal + part
            start = (blocks - shift) * BLOCK
            if seq == 0:
                sum_ref[head, :, start : start + BLOCK] = diagonal
            else:
                sum_ref[head, :, start : start + BLOCK] += diagonal
        grad_low = grad_s.astype(BF16)
        grad_v = grad_v + nn(probs.astype(BF16), own_up)
        grad_k = grad_k + nn(grad_low, own)
        keys_t = k_ref[span, :].T[head * head_width : (head + 1) * head_width]
        grad_q.append(nn(keys_t, grad_low))
        if head == per - 1:
            dq_ref[span, :] = (jnp.concatenate(grad_q, axis=0).T * scale).astype(BF16)
            dk_ref[span, :] = grad_k.astype(BF16)
            dv_ref[span, :] = grad_v.astype(BF16)
            grad_q, grad_k, grad_v = [], 0.0, 0.0
    for head in range(per):
        sum_ref[head, :, 0:BLOCK] = jnp.zeros((BLOCK, BLOCK), F32)
        diag_ref[0, head : head + 1, :] = fold(sum_ref[head])


def attend_back(
    seq_len, rel_bias, desc, queries, keys, values, grad_heads, lse, head_width, scale, first_pair, pairs
):
    rows = queries.shape[0]
    width = pairs * LANES
    per = LANES // head_width
    span = desc.shape[1]
    length = rows // seq_len.shape[0]
    taken = pl.BlockSpec((rows, LANES), lambda i: (0, i + first_pair))
    block = pl.BlockSpec((rows, LANES), lambda i: (0, i))
    return pl.pallas_call(
        functools.partial(attend_back_kernel, head_width, scale, first_pair),
        grid=(pairs,),
        in_specs=[
            smem(), smem(), whole(desc.shape), taken, taken, taken, taken,
            pl.BlockSpec((1, per, rows), lambda i: (i + first_pair, 0, 0)),
        ],
        out_specs=[block, block, block, pl.BlockSpec((1, per, span), lambda i: (i, 0, 0))],
        out_shape=[out((rows, width), BF16)] * 3 + [out((pairs, per, span), F32)],
        scratch_shapes=[pltpu.VMEM((per, BLOCK, span), F32)] * 2,
        compiler_params=params(),
        cost_estimate=cost(rows * length * width, rows * width),
        name="attend_back",
    )(seq_len, rel_bias, desc, queries, keys, values, grad_heads, lse)


def wide_router(router):
    first = router.astype(BF16)
    second = (router - first.astype(F32)).astype(BF16)
    rest = jnp.zeros((LANES - router.shape[0], router.shape[1]), F32)
    return [
        jnp.concatenate([part.astype(F32), rest], axis=0).astype(BF16) for part in (first, second)
    ]


def router_probs(normed, router, expert_count):
    both = nt(normed, jnp.concatenate(wide_router(router), axis=0))
    logits = both[:, :LANES] + both[:, LANES:]
    lanes = lax.broadcasted_iota(jnp.int32, logits.shape, 1)
    logits = jnp.where(lanes < expert_count, logits, -jnp.inf)
    expo = jnp.exp(logits - jnp.max(logits, axis=-1, keepdims=True))
    return expo / jnp.sum(expo, axis=-1, keepdims=True)


def middle_kernel(
    expert_count, steps, slot_tile, len_ref, attn_ref, x_ref, w_ref, gain_ref, router_ref, slot_ref,
    mid_ref, probs_ref, sums_ref, buffer_a_ref, buffer_b_ref, normed_all,
):
    step = pl.program_id(0)
    tile = attn_ref.shape[0]
    rows = slot_ref.shape[1]
    seq_count = len_ref.shape[0]

    @pl.when(step == 0)
    def _():
        sums_ref[...] = jnp.zeros_like(sums_ref)

    @pl.when(step < steps)
    def _():
        middle = x_ref[...].astype(F32) + nn(attn_ref[...], w_ref[...])
        mid_ref[...] = middle.astype(BF16)
        normed = (middle * factor_of(middle) * gain_ref[...][None, :]).astype(BF16)
        normed_all[pl.ds(pl.multiple_of(step * tile, tile), tile), :] = normed
        probs = router_probs(normed, router_ref[...], expert_count)
        probs_ref[...] = probs
        valid = valid_rows(len_ref, step * tile, tile, rows // seq_count, seq_count)
        sums_ref[...] += jnp.sum(jnp.where(valid, probs, 0.0), axis=0, keepdims=True)

    @pl.when(step >= steps)
    def _():
        slots = lax.broadcasted_iota(jnp.int32, (slot_tile, rows), 0) + (step - steps) * slot_tile
        pick = jnp.where(slot_ref[...] == slots, 1.0, 0.0).astype(BF16)
        picked = nn(pick, normed_all[...]).astype(BF16)

        @pl.when(step < steps + 2)
        def _():
            buffer_a_ref[...] = picked

        @pl.when(step >= steps + 2)
        def _():
            buffer_b_ref[...] = picked


def middle_of(seq_len, attn, tokens, w_out_proj, gain, router, slot_row, expert_count, slots):
    rows, width = attn.shape
    tile, slot_tile = 256, slots // 4
    steps = rows // tile
    block = pl.BlockSpec((tile, width), lambda i: (jnp.minimum(i, steps - 1), 0))
    return pl.pallas_call(
        functools.partial(middle_kernel, expert_count, steps, slot_tile),
        grid=(steps + 4,),
        in_specs=[
            smem(), block, block, whole((width, width)), whole((width,)), whole((expert_count, width)),
            whole((1, rows)),
        ],
        out_specs=[
            block,
            pl.BlockSpec((tile, LANES), lambda i: (jnp.minimum(i, steps - 1), 0)),
            whole((1, LANES)),
        ] + halves(slot_tile, width, steps, 2),
        out_shape=[
            out((rows, width), BF16), out((rows, LANES), F32), out((1, LANES), F32),
            out((slots // 2, width), BF16), out((slots // 2, width), BF16),
        ],
        scratch_shapes=[pltpu.VMEM((rows, width), BF16)],
        compiler_params=params(),
        cost_estimate=cost(
            2 * rows * width * (width + slots), 2 * width * (4 * rows + slots + width)
        ),
        name="middle",
    )(seq_len, attn, tokens, w_out_proj, gain, router, slot_row)


def gelu_pair(hidden):
    root = 0.7978845608028654
    square = hidden * hidden
    half = 0.5 + 0.5 * jnp.tanh(hidden * (root + (root * 0.044715) * square))
    bend = (1.0 - half) * (hidden * (2.0 * root + (6.0 * 0.044715 * root) * square))
    return hidden * half, half + half * bend


def expert_kernel(
    expert_count, me_ref, x_ref, g_ref, w_in_ref, w_out_ref, router_ref, *refs
):
    (
        result_ref, back_ref, active_ref, grad_ref, grad_rows_ref, grad_router_ref,
        result_sum, back_sum, probs_all,
    ) = refs[-9:]
    expert_step(
        expert_count, me_ref, x_ref, g_ref, w_in_ref, w_out_ref, router_ref,
        result_ref, back_ref, active_ref, grad_ref, grad_rows_ref, grad_router_ref,
        result_sum, back_sum, probs_all,
    )


def expert_step(
    expert_count, me_ref, x_ref, g_ref, w_in_ref, w_out_ref, router_ref,
    result_ref, back_ref, active_ref, grad_ref, grad_rows_ref, grad_router_ref,
    result_sum, back_sum, probs_all,
):
    step = pl.program_id(0)
    last = pl.num_programs(0) - 1
    rows = x_ref.shape[0]
    tile = rows // 2
    me = me_ref[0]
    lanes = lax.broadcasted_iota(jnp.int32, (1, LANES), 1)
    sources = g_ref.shape[0] // 2

    def cot(low):
        first = low // tile * sources
        return g_ref[first : first + sources].reshape(tile, -1).astype(F32)

    @pl.when(step == 0)
    def _():
        result_sum[...] = jnp.zeros_like(result_sum)
        back_sum[...] = jnp.zeros_like(back_sum)
        for low in range(0, rows, tile):
            probs = router_probs(x_ref[low : low + tile, :], router_ref[...], expert_count)
            probs_all[low : low + tile, :] = probs
            gate = jnp.sum(jnp.where(lanes == me, probs, 0.0), axis=1, keepdims=True)
            grad_rows_ref[low : low + tile, :] = (gate * cot(low)).astype(BF16)

    parts = [slice(low, low + tile) for low in range(0, rows, tile)]
    ahead = []
    for part in parts:
        hidden = nn(x_ref[part, :], w_in_ref[...])
        ahead.append((hidden, nt(grad_rows_ref[part, :], w_out_ref[...])))
    for part, (hidden, upstream) in zip(parts, ahead):
        active, slope = gelu_pair(hidden)
        active = active.astype(BF16)
        grad = (upstream * slope).astype(BF16)
        active_ref[part, :] = active
        grad_ref[part, :] = grad
        result_sum[part, :] += nn(active, w_out_ref[...])
        back_sum[part, :] += nt(grad, w_in_ref[...])

    @pl.when(step == last)
    def _():
        total = jnp.zeros(grad_router_ref.shape, F32)
        for low in range(0, rows, tile):
            part = slice(low, low + tile)
            result = result_sum[part, :].astype(BF16)
            first = low // tile * sources
            result_ref[first : first + sources] = result.reshape(sources, -1, result.shape[1])
            grad_gate = jnp.sum(cot(low) * result.astype(F32), axis=1, keepdims=True)
            probs = probs_all[part, :]
            own = lanes == me
            gate = jnp.sum(jnp.where(own, probs, 0.0), axis=1, keepdims=True)
            grad_logits = (grad_gate * probs * (jnp.where(own, 1.0, 0.0) - gate)).astype(BF16)
            back_ref[part, :] = (
                back_sum[part, :] + nn(grad_logits, wide_router(router_ref[...])[0])
            ).astype(BF16)
            total = total + tn(grad_logits, x_ref[part, :])[:expert_count]
        grad_router_ref[...] = total


def expert(me, received, grad_rows, w_in, w_out, router, expert_count, chunk, chunks, before):
    rows, width = received.shape
    sources, capacity = grad_rows.shape[0], grad_rows.shape[1]
    hidden = w_in.shape[1]
    tile = 512
    part = capacity // chunks
    direct = part % 16 == 0
    if not direct:
        grad_rows = grad_rows[:, chunk * part : (chunk + 1) * part]
    place = chunk if direct else 0
    piece = pl.BlockSpec((sources, part, width), lambda i: (0, place, 0))
    operands = [me, received, grad_rows, w_in, w_out, router]
    in_specs = [
        smem(), whole((rows, width)), piece,
        pl.BlockSpec((width, tile), lambda i: (0, i)),
        pl.BlockSpec((tile, width), lambda i: (i, 0)),
        whole((expert_count, width)),
    ]
    aliases = {}
    if direct and before is not None:
        aliases = {len(operands): 0}
        operands.append(before)
        in_specs.append(pl.BlockSpec(memory_space=pl.ANY))
    result, *rest = pl.pallas_call(
        functools.partial(expert_kernel, expert_count),
        grid=(hidden // tile,),
        in_specs=in_specs,
        out_specs=[
            piece, whole((rows, width)),
            pl.BlockSpec((rows, tile), lambda i: (0, i)),
            pl.BlockSpec((rows, tile), lambda i: (0, i)),
            whole((rows, width)),
            whole((expert_count, width)),
        ],
        out_shape=[
            out(grad_rows.shape, BF16), out((rows, width), BF16), out((rows, hidden), BF16),
            out((rows, hidden), BF16), out((rows, width), BF16), out((expert_count, width), F32),
        ],
        scratch_shapes=[
            pltpu.VMEM((rows, width), F32), pltpu.VMEM((rows, width), F32),
            pltpu.VMEM((rows, LANES), F32),
        ],
        input_output_aliases=aliases,
        compiler_params=params(),
        cost_estimate=cost(16 * rows * width * hidden, 4 * rows * (hidden + 2 * width)),
        name="expert",
    )(*operands)
    if not direct and before is not None:
        result = jnp.concatenate([before, result], axis=1)
    return result, *rest


def grad_w_out_kernel(active_a_ref, active_b_ref, g_a_ref, g_b_ref, out_ref):
    grad = tn(active_a_ref[...], g_a_ref[...]) + tn(active_b_ref[...], g_b_ref[...])
    out_ref[...] = grad.astype(BF16)


def grad_w_in_kernel(grad_a_ref, grad_b_ref, x_a_ref, x_b_ref, out_ref, turned):
    rows = x_a_ref.shape[0]

    @pl.when(pl.program_id(0) == 0)
    def _():
        turned[:, 0:rows] = x_a_ref[...].T
        turned[:, rows:] = x_b_ref[...].T

    grad = nn(turned[:, 0:rows], grad_a_ref[...]) + nn(turned[:, rows:], grad_b_ref[...])
    out_ref[...] = grad.astype(BF16)


def grad_of_expert(kernel, moving, still, shares, turned, name):
    rows, width = still[0].shape
    hidden = moving[0].shape[1]
    part = hidden // shares
    shape = (width, part) if turned else (part, width)
    block = pl.BlockSpec((rows, part), lambda i: (0, i))
    return pl.pallas_call(
        kernel,
        grid=(shares,),
        in_specs=[block] * 2 + [whole((rows, width))] * 2,
        out_specs=pl.BlockSpec((None, *shape), lambda i: (i, 0, 0)),
        out_shape=out((shares, *shape), BF16),
        scratch_shapes=[pltpu.VMEM((width, 2 * rows), BF16)] * turned,
        compiler_params=params(),
        cost_estimate=cost(8 * rows * width * hidden, 2 * (2 * rows + width) * (hidden + width)),
        name=name,
    )(*moving, *still)


def gather_rows(slot_ref, tile, *refs):
    rows = refs[0].shape[0]
    total = None
    for index, ref in enumerate(refs):
        slots = lax.broadcasted_iota(jnp.int32, (tile, rows), 1) + index * rows
        pick = jnp.where(slot_ref[...] == slots, 1.0, 0.0).astype(BF16)
        more = nn(pick, ref[...])
        total = more if total is None else total + more
    return total


def combine_back_kernel(
    balance_scale, expert_count, len_ref, back_a_ref, back_b_ref, slot_ref, cot_ref, mid_ref, probs_ref,
    w_ref, router_ref, gain_ref, counts_ref, rows_total,
    branch_ref, heads_ref, grad_gain_ref, grad_router_ref,
):
    step = pl.program_id(0)
    tile = mid_ref.shape[0]
    seq_count = len_ref.shape[0]
    probs = probs_ref[...]
    valid = valid_rows(len_ref, step * tile, tile, rows_total // seq_count, seq_count)
    pull = jnp.where(valid, counts_ref[0:1, :] * balance_scale, 0.0)
    grad_logits = (probs * (pull - jnp.sum(probs * pull, axis=1, keepdims=True))).astype(BF16)
    grad_normed = gather_rows(slot_ref, tile, back_a_ref, back_b_ref)
    grad_normed = grad_normed + nn(grad_logits, wide_router(router_ref[...])[0])
    middle = mid_ref[...].astype(F32)
    factor = factor_of(middle)
    gain = gain_ref[...][None, :]
    normed = (middle * factor * gain).astype(BF16)
    grad_mid, grad_gain = norm_back(middle, factor, gain, grad_normed)
    grad_mid = grad_mid + cot_ref[...].astype(F32)
    branch = grad_mid.astype(BF16)
    branch_ref[...] = branch
    heads_ref[...] = nt(branch, w_ref[...]).astype(BF16)
    grad_router = tn(grad_logits, normed)[:expert_count]

    @pl.when(step == 0)
    def _():
        grad_gain_ref[...] = grad_gain
        grad_router_ref[...] = grad_router

    @pl.when(step > 0)
    def _():
        grad_gain_ref[...] += grad_gain
        grad_router_ref[...] += grad_router


def combine_back(
    seq_len, back, slot_col, cotangent, middle, probs, w_out_proj, router, gain, counts, balance_scale
):
    rows, width = middle.shape
    slots = 2 * back[0].shape[0]
    expert_count = router.shape[0]
    tile = 512
    block = pl.BlockSpec((tile, width), lambda i: (i, 0))

    def kernel(*refs):
        combine_back_kernel(balance_scale, expert_count, *refs[:11], rows, *refs[11:])

    return pl.pallas_call(
        kernel,
        grid=(rows // tile,),
        in_specs=[
            smem(), whole((slots // 2, width)), whole((slots // 2, width)),
            pl.BlockSpec((tile, 1), lambda i: (i, 0)), block, block,
            pl.BlockSpec((tile, LANES), lambda i: (i, 0)), whole((width, width)),
            whole((expert_count, width)), whole((width,)), whole((8, LANES)),
        ],
        out_specs=[block, block, whole((1, width)), whole((expert_count, width))],
        out_shape=[
            out((rows, width), BF16), out((rows, width), BF16),
            out((1, width), F32), out((expert_count, width), F32),
        ],
        compiler_params=params(),
        cost_estimate=cost(
            rows * width, rows * width
        ),
        name="combine_back",
    )(seq_len, *back, slot_col, cotangent, middle, probs, w_out_proj, router, gain, counts)


def output_kernel(expert_count, back_ref, slot_ref, mid_ref, probs_ref, out_ref):
    tile = mid_ref.shape[0]
    capacity = back_ref.shape[0] // expert_count
    combined = gather_rows(slot_ref, tile, back_ref)
    first = lax.broadcasted_iota(jnp.int32, (tile, LANES), 1) * capacity
    slot = slot_ref[...]
    own = (slot >= first) & (slot < first + capacity)
    gate = jnp.sum(jnp.where(own, probs_ref[...], 0.0), axis=1, keepdims=True)
    out_ref[...] = (mid_ref[...].astype(F32) + gate * combined).astype(BF16)


def layer_output(returned, slot_col, middle, probs, expert_count):
    rows, width = middle.shape
    slots = returned.shape[0]
    tile = 256
    block = pl.BlockSpec((tile, width), lambda i: (i, 0))
    thin = pl.BlockSpec((tile, 1), lambda i: (i, 0))
    return pl.pallas_call(
        functools.partial(output_kernel, expert_count),
        grid=(rows // tile,),
        in_specs=[
            whole((slots, width)), thin, block, pl.BlockSpec((tile, LANES), lambda i: (i, 0)),
        ],
        out_specs=block,
        out_shape=out((rows, width), BF16),
        compiler_params=params(),
        cost_estimate=cost(2 * rows * width * slots, 2 * width * (3 * rows + slots)),
        name="layer_output",
    )(returned, slot_col, middle, probs)


def grad_weights_kernel(counts, core_ref, *refs):
    lefts, refs = refs[: len(counts)], refs[len(counts) :]
    rights, refs = refs[: sum(counts)], refs[sum(counts) :]
    (keep_ref, send_ref), turned = refs[:2], refs[2:]
    half, tile = keep_ref.shape[1], keep_ref.shape[2]

    @pl.when(pl.program_id(0) == 0)
    def _():
        for left, scratch in zip(lefts, turned):
            scratch[...] = left[...].T

    for index, result in enumerate((keep_ref, send_ref)):
        side = core_ref[0] if index == 0 else 1 - core_ref[0]
        done = 0
        for count, scratch in zip(counts, turned):
            left = scratch[pl.ds(pl.multiple_of(side * half, half), half), :]
            right = jnp.concatenate([ref[...] for ref in rights[done : done + count]], axis=1)
            product = nn(left, right).astype(BF16)
            for place in range(count):
                result[done + place] = product[:, place * tile : (place + 1) * tile]
            done += count


def grad_of_weights(core, pairs, span):
    rows, width = pairs[0][0].shape
    counts = tuple(len(rights) for _, rights in pairs)
    tile = 128
    result = pl.BlockSpec((sum(counts), width // 2, tile), lambda i: (0, 0, i))
    lefts = [left for left, _ in pairs]
    rights = [right for _, some in pairs for right in some]
    total = out((sum(counts), width // 2, span), BF16)
    return pl.pallas_call(
        functools.partial(grad_weights_kernel, counts),
        grid=(span // tile,),
        in_specs=[smem()] + [whole((rows, width))] * len(lefts) + [
            pl.BlockSpec((rows, tile), lambda i, first=first // tile: (0, i + first)) for _, first in rights
        ],
        out_specs=[result, result],
        out_shape=[total, total],
        scratch_shapes=[pltpu.VMEM((width, rows), BF16)] * len(lefts),
        compiler_params=params(),
        cost_estimate=cost(
            rows * width, rows * width
        ),
        name="grad_weights",
    )(core, *lefts, *[right for right, _ in rights])


def add_split_kernel(me_ref, keep_ref, got_ref, *outs):
    total = (keep_ref[...].astype(F32) + got_ref[...].astype(F32)).astype(BF16)
    for index, ref in enumerate(outs):

        @pl.when(pl.program_id(0) == index)
        def _(ref=ref):
            ref[...] = total


def add_split(me, keep, got, shares):
    rows, span = keep.shape
    piece = rows // shares
    block = pl.BlockSpec((None, piece, span), lambda i, me: (me[0] ^ i, 0, 0))
    return pl.pallas_call(
        add_split_kernel,
        grid_spec=pltpu.PrefetchScalarGridSpec(
            num_scalar_prefetch=1,
            grid=(shares,),
            in_specs=[block, block],
            out_specs=[whole((piece, span))] * shares,
        ),
        out_shape=[out((piece, span), BF16)] * shares,
        compiler_params=params(),
        cost_estimate=cost(rows * span, 8 * rows * span),
        name="add_split",
    )(me, keep.reshape(shares, piece, span), got.reshape(shares, piece, span))


def grad_tokens_kernel(groups, *refs):
    grad_refs, (w_ref, x_ref, gain_ref, mid_ref, out_ref, grad_gain_ref) = refs[: 3 * groups], refs[3 * groups :]
    step = pl.program_id(0)
    width = x_ref.shape[1]
    span = width // groups
    upstream = 0.0
    for group in range(groups):
        for part in range(3):
            start = part * width + group * span
            upstream = upstream + nt(grad_refs[3 * group + part][...], w_ref[:, start : start + span])
    values = x_ref[...].astype(F32)
    grad, grad_gain = norm_back(values, factor_of(values), gain_ref[...][None, :], upstream)
    out_ref[...] = mid_ref[...].astype(F32) + grad

    @pl.when(step == 0)
    def _():
        grad_gain_ref[...] = grad_gain

    @pl.when(step > 0)
    def _():
        grad_gain_ref[...] += grad_gain


def grad_of_tokens(grads, w_qkv, tokens, gain, grad_mid):
    rows, width = tokens.shape
    groups = len(grads) // 3
    tile = 512
    block = pl.BlockSpec((tile, width), lambda i: (i, 0))
    taken = pl.BlockSpec((tile, width // groups), lambda i: (i, 0))
    return pl.pallas_call(
        functools.partial(grad_tokens_kernel, groups),
        grid=(rows // tile,),
        in_specs=[taken] * len(grads) + [whole((width, 3 * width)), block, whole((width,)), block],
        out_specs=[block, whole((1, width))],
        out_shape=[out((rows, width), F32), out((1, width), F32)],
        compiler_params=params(),
        cost_estimate=cost(rows * width, rows * width),
        name="grad_tokens",
    )(*grads, w_qkv, tokens, gain, grad_mid)


def after(value, *earlier):
    return lax.optimization_barrier((value, *earlier))[0]


def swap(value, axis, mask):
    return lax.ppermute(value, axis, [(i, i ^ mask) for i in range(lax.axis_size(axis))])


def tree(parts):
    parts = [part.astype(F32) for part in parts]
    while len(parts) > 1:
        parts = [parts[i] + parts[i + 1] for i in range(0, len(parts), 2)]
    return parts[0]


class Group:
    def __init__(self, axis, shift, size):
        self.axis, self.shift, self.size = axis, shift, size
        self.index = (lax.axis_index(axis) >> shift) % size

    def swaps(self, of):
        return [swap(of(d), self.axis, d << self.shift) for d in range(1, self.size)]

    def total(self, value):
        return tree([value] + self.swaps(lambda d: value))

    def doubled(self, value, bit):
        while bit < self.size:
            value = tree([value, swap(value, self.axis, bit << self.shift)]).astype(value.dtype)
            bit *= 2
        return value

    def parts(self, pieces):
        return [pieces[0]] + self.swaps(lambda d: pieces[d])

    def gather(self, value):
        parts = [value] + self.swaps(lambda d: value)
        bit = 1
        while bit < self.size:
            flip = (self.index & bit) != 0
            parts = [jnp.where(flip, parts[j ^ bit], parts[j]) for j in range(self.size)]
            bit *= 2
        return jnp.stack(parts)


def gather_pieces(piece, shape, core, data):
    return core.gather(data.gather(piece).reshape(shape))


def body(
    tokens,
    cotangent,
    routes,
    seq_len,
    buckets,
    w_qkv,
    w_out_proj,
    rel_bias,
    gain_attn,
    gain_ffn,
    router,
    w_in,
    w_out,
):
    rows, width = tokens.shape
    bucket_count, heads_count = rel_bias.shape
    head_width = width // heads_count
    expert_count = router.shape[1]
    capacity = max(2, (5 * rows + 4 * expert_count - 1) // (4 * expert_count))
    slots = expert_count * capacity
    shares, experts_axis = lax.axis_size("dp"), lax.axis_size("expert")
    token_total = float(rows * shares * experts_axis)
    scale = head_width ** (-0.5)
    first_mat, second_mat = w_in[0], w_out[0]
    router_t, rel_t = router.T, rel_bias.T
    me = lax.axis_index("expert").astype(jnp.int32)[None]
    me_dp = lax.axis_index("dp").astype(jnp.int32)[None]
    core = Group("expert", 0, 2)
    line = Group("expert", 1, experts_axis // 2)
    data = Group("dp", 0, shares)

    def exchange(array):
        return lax.all_to_all(array, "expert", split_axis=0, concat_axis=0, tiled=True)

    def sum_small(array):
        return line.total(data.total(core.total(array)))

    grad_rows, slot_col, slot_plain, slot_row, counts, desc = route(
        seq_len, routes.T, buckets, cotangent, expert_count, capacity
    )
    grad_rows = exchange(grad_rows)
    counts = sum_small(counts)

    normed_a, queries, keys, values = project_qkv(tokens, gain_attn, w_qkv, scale)
    attn, lse = attend(seq_len, rel_t, desc, queries, keys, values, head_width)
    middle, probs, prob_sums, *buffer = middle_of(
        seq_len, attn, tokens, w_out_proj, gain_ffn, router_t, slot_row, expert_count, slots
    )
    buffer[0], buffer[1], grad_rows = lax.optimization_barrier((*buffer, grad_rows))
    received = [exchange(part) for part in buffer]
    received[0], counts = lax.optimization_barrier((received[0], counts))
    grad_rows = grad_rows.reshape(experts_axis, -1, width)
    result, done = None, []
    for chunk in range(2):
        result, *rest = expert(
            me, received[chunk], grad_rows, first_mat, second_mat, router_t, expert_count, chunk, 2, result
        )
        done.append(rest)
    back, active, grad_hidden, grad_result, grad_router_e = zip(*done)
    first_back = exchange(back[0])
    back = [first_back, exchange(after(back[1], first_back))]

    def scatter_shares(grad):
        return lax.psum_scatter(grad, "dp", scatter_dimension=0, tiled=True)

    active, back[0] = lax.optimization_barrier((active, back[0]))
    grad_second = grad_of_expert(grad_w_out_kernel, active, grad_result, shares, 0, "grad_w_out")
    grad_hidden, grad_second = lax.optimization_barrier((grad_hidden, grad_second))
    grad_first = grad_of_expert(grad_w_in_kernel, grad_hidden, received, shares, 1, "grad_w_in")
    back[1], grad_first = lax.optimization_barrier((back[1], grad_first))
    grad_second = scatter_shares(grad_second)
    grad_first = scatter_shares(grad_first)

    branch, grad_heads, grad_gain_b, grad_router_t = combine_back(
        seq_len, back, slot_col, cotangent, middle, probs, w_out_proj, router_t, gain_ffn, counts,
        AUX_WEIGHT * expert_count / token_total / token_total,
    )
    returned = exchange(after(result.reshape(slots, width), grad_heads))
    grad_router = grad_router_e[0] + grad_router_e[1] + grad_router_t
    core_index = me & 1

    groups = 2
    pairs = width // LANES // groups
    span = pairs * LANES
    grads, diags, sums = [], [], []
    for group in range(groups):
        *some, diag = attend_back(
            seq_len, rel_t, desc, queries, keys, values, grad_heads, lse, head_width, scale,
            group * pairs, pairs,
        )
        grads += some
        diags.append(diag.reshape(heads_count // groups, -1))
        products = [(normed_a, [(part, 0) for part in some])]
        if group == 1:
            some, got, grad_second = lax.optimization_barrier((some, got, grad_second))
            pieces = add_split(me_dp, keep.reshape(-1, span), got.reshape(-1, span), shares)
            *some, own = lax.optimization_barrier((*some, pieces[0]))
            pieces = [own, *pieces[1:]]
            products = [(normed_a, [(part, 0) for part in some])]
        if group == 0:
            products.append((attn, [(branch, first) for first in range(0, width, span)]))
            keep, send = grad_of_weights(core_index, products, span)
            got = swap(send, "expert", 1)
            grad_heads, keep = lax.optimization_barrier((grad_heads, keep))
            shape = keep.shape
        else:
            keep, send = grad_of_weights(core_index, products, span)
            got = swap(send, "expert", 1)
            parts = data.parts(pieces)
            grads, keep, returned = lax.optimization_barrier((grads, keep, returned))
            grad_tokens, grad_gain_a = grad_of_tokens(grads, w_qkv, tokens, gain_attn, branch)
            grad_tokens, parts, got, grad_first = lax.optimization_barrier((grad_tokens, parts, got, grad_first))
            piece = tree(parts).astype(BF16)
            moved = swap(piece, line.axis, 2)
            pieces = add_split(me_dp, keep.reshape(-1, span), got.reshape(-1, span), shares)
            onehot = (desc == jnp.arange(bucket_count, dtype=jnp.int32)[:, None]).astype(F32)
            grad_rel = dot(onehot, jnp.concatenate(diags, axis=0), ((1,), (1,)), HIGHEST)
            small = [grad_gain_a, grad_gain_b, grad_router, prob_sums, grad_rel]
            packed = jnp.concatenate([part.reshape(-1) for part in small]).reshape(-1, LANES)
            packed = core.total(packed)
            returned, own, packed = lax.optimization_barrier((returned, pieces[0], packed))
            packed = data.parts([packed] * shares)
            parts = data.parts([own, *pieces[1:]])
            output = layer_output(returned, slot_plain, middle, probs, expert_count)
            grad_first, grad_second = grad_first.astype(F32), grad_second.astype(F32)
            output, moved, parts, packed, grad_first, grad_second = lax.optimization_barrier(
                (output, moved, parts, packed, grad_first, grad_second)
            )
            piece = line.doubled(tree([piece, moved]).astype(BF16), 2)
            sums.append(gather_pieces(piece, shape, core, data))
            piece = line.doubled(tree(parts).astype(BF16), 1)
            packed = line.parts([tree(packed)] * line.size)
            piece, packed = lax.optimization_barrier((piece, packed))
            sums.append(gather_pieces(piece, keep.shape, core, data))

    packed = tree(packed)
    packed, summed = packed.reshape(-1), []
    for part in small:
        summed.append(packed[: part.size].reshape(part.shape))
        packed = packed[part.size :]
    balance = expert_count * jnp.sum((counts[0] / token_total) * (summed[3][0] / token_total))

    def both_halves(columns):
        rows_of = [jnp.concatenate([part[half, i] for part, i in columns], axis=1) for half in range(2)]
        return jnp.concatenate(rows_of, axis=0).astype(F32)

    grad_qkv = both_halves([(sums[g], i) for i in range(3) for g in range(groups)])
    grad_proj = both_halves([(sums[0], 3 + g) for g in range(groups)])
    return (
        output,
        grad_tokens,
        grad_qkv,
        grad_proj,
        summed[4],
        summed[0][0],
        summed[1][0],
        summed[2].T,
        grad_first,
        grad_second,
        balance,
    )


def solution(mesh):
    placed = (
        P(("dp", "expert"), None),
        P(("dp", "expert"), None),
        P(("dp", "expert"), None),
        P(("dp", "expert")),
        P(),
        P(),
        P(),
        P(),
        P(),
        P(),
        P(),
        P("expert", None, None),
        P("expert", None, None),
    )
    return jax.shard_map(
        body,
        mesh=mesh,
        in_specs=placed,
        out_specs=(
            P(("dp", "expert"), None),
            P(("dp", "expert"), None),
            P(),
            P(),
            P(),
            P(),
            P(),
            P(),
            P("expert", None, "dp"),
            P("expert", "dp", None),
            P(),
        ),
        check_vma=False,
    )
```
